768 devices in a mesh: row: 32 (over x, z_lo, core), col: 24 (over z_hi, y).
Axes of the slice: x: 4, y: 8, z: 12 (z_hi: 3, z_lo: 4; z = z_hi * 4 + z_lo), core: 2. Of those that a mesh axis runs over, the one named last changes fastest.
Arguments:
- x_blocks: float32 [1536, 4, 128, 128], P(('row', 'col')), may hold values from -2.5 to 2.5
- x_cols: int32 [1536, 4], replicated, may hold values from 0 to 1535, as said below
- mask_cols: int32 [1536, 6], replicated, may hold values from 0 to 1535, as said below
- mask_count: int32 [1536], replicated, may hold values from 4 to 6
Outputs:
- square: float32 [1536, 6, 128, 128], P(('row', 'col'))
- x_cubed: float32 [1536, 6, 128, 128], P(('row', 'col'))
The draws below stay inside these ranges and needn't reach their ends.
Inputs may be any that keep to these rules, and one draw needn't show every extreme that they name: `x_cols`: slot 0 of block row i is i itself; slots 1, 2 and 3 are the cell positions one step away from i, periodically, along the first, second and third dimension of the cell respectively, each in a direction of its own. `mask_cols`: the 6 product columns of block row i are distinct cell positions at offsets from i among (0,0,0), (1,0,0), (-1,0,0), (2,0,0), (0,1,0), (0,-1,0), (0,2,0), (0,0,1), periodically, in any order; slots past mask_count also hold such columns.
All inputs are finite; a program needn't handle non-finite values.
Results may differ from the reference program's by a relative error of at most 0.0003.
Values sent between devices are 32-bit elements; how exact they have to be, the bound alone decides.
No kernel may reach another device: no remote copies, remote signals or barrier semaphores. Data moves between devices by JAX's collectives and lax.ppermute only.
A program may use at most 32 MiB of HBM per device.

```python
import jax
import jax.numpy as jnp
from jax import lax

BS = 128
SLOTS = 4
MSLOTS = 6
GX = 48
GZ = 8
NB = 1536


def cell_column(first, second, third):
    return (jnp.mod(first, GX) + GX * (jnp.mod(second, 4) + 4 * jnp.mod(third, GZ))).astype(jnp.int32)


def cell_coords():
    row_numbers = jnp.arange(NB, dtype=jnp.int32)
    first = jnp.mod(row_numbers, GX)
    second = jnp.mod(row_numbers // GX, 4)
    third = row_numbers // (GX * 4)
    return (first, second, third)


def draw_x_cols(key, part):
    key = jax.random.fold_in(key, 11)
    signs = 2 * jax.random.randint(key, (NB, 3), 0, 2) - 1
    first, second, third = cell_coords()
    own = cell_column(first, second, third)
    step_one = cell_column(first + signs[:, 0], second, third)
    step_two = cell_column(first, second + signs[:, 1], third)
    step_three = cell_column(first, second, third + signs[:, 2])
    return jnp.stack([own, step_one, step_two, step_three], axis=1).astype(jnp.int32)


def draw_mask_cols(key, part):
    key = jax.random.fold_in(key, 12)
    row_keys = jax.random.split(key, NB)
    shuffled = jax.vmap(lambda one_key: jax.random.permutation(one_key, 8))(row_keys)[:, :MSLOTS]
    table_first = jnp.array([0, 1, -1, 2, 0, 0, 0, 0], dtype=jnp.int32)
    table_second = jnp.array([0, 0, 0, 0, 1, -1, 2, 0], dtype=jnp.int32)
    table_third = jnp.array([0, 0, 0, 0, 0, 0, 0, 1], dtype=jnp.int32)
    first, second, third = cell_coords()
    move_first = jnp.take(table_first, shuffled)
    move_second = jnp.take(table_second, shuffled)
    move_third = jnp.take(table_third, shuffled)
    return cell_column(first[:, None] + move_first, second[:, None] + move_second, third[:, None] + move_third)


def draw_mask_count(key, part):
    key = jax.random.fold_in(key, 13)
    first_key, second_key = jax.random.split(key)
    counts = jax.random.randint(first_key, (NB,), 4, MSLOTS + 1)
    chosen_row = jax.random.randint(second_key, (), 0, NB)
    counts = counts.at[chosen_row].set(MSLOTS)
    counts = counts.at[jnp.mod(chosen_row + NB // 2, NB)].set(4)
    return counts.astype(jnp.int32)


def level_of(rng, shape, pieces, least, high):
    loudness = 1.0
    for dim, blocks in pieces:
        steps = jax.random.uniform(jax.random.fold_in(jax.random.fold_in(rng, 6), dim), (blocks,), jnp.float32, least / len(pieces), high / len(pieces))
        loudness = loudness * jnp.repeat(jnp.exp(steps), shape[dim] // blocks).reshape((-1,) + (1,) * (len(shape) - 1 - dim))
    return loudness


def normal_values(stream_key, extent, deviation, limit, cuts=(), kind=jnp.bfloat16):
    values = deviation * jax.random.normal(stream_key, extent, jnp.float32)
    if cuts:
        values = values * level_of(stream_key, extent, cuts, -0.22, 0.18)
    return jnp.clip(values, -limit, limit).astype(kind)


def setup_inputs(seed: int = 0) -> dict:
    key_of = jax.random.split(jax.random.key(seed), 5)
    return {
        "x_blocks": normal_values(key_of[0], (NB, SLOTS, BS, BS), 0.25, 2.5, ((0, 768),), jnp.float32),
        "x_cols": draw_x_cols(jax.random.fold_in(key_of[4], 71), 0),
        "mask_cols": draw_mask_cols(jax.random.fold_in(key_of[4], 71), 0),
        "mask_count": draw_mask_count(jax.random.fold_in(key_of[4], 71), 0),
    }


def pick_product(a_vals, pool_row, block_pool, b_cols, out_cols, live_mask):
    pool_rows = b_cols.shape[0]
    pool_slots = b_cols.shape[1]
    row_columns = jnp.take(b_cols, pool_row, axis=0)
    matches = row_columns[:, None, :, :] == out_cols[:, :, None, None]
    present = jnp.any(matches, axis=-1)
    slot_index = jnp.sum(jnp.where(matches, jnp.arange(pool_slots, dtype=jnp.int32), 0), axis=-1).astype(jnp.int32)
    flat_index = jnp.where(present, pool_row[:, None, :] * pool_slots + slot_index, pool_rows * pool_slots).astype(jnp.int32)
    picked = jnp.take(block_pool, flat_index, axis=0)
    products = jnp.einsum('rsij,rmsjk->rmik', a_vals, picked, precision=lax.Precision.HIGHEST, preferred_element_type=jnp.float32)
    return products * live_mask[:, :, None, None].astype(jnp.float32)


def add_empty(values):
    block_size = values.shape[-1]
    flat_blocks = values.reshape(values.shape[0] * values.shape[1], block_size, block_size)
    return jnp.concatenate([flat_blocks, jnp.zeros((1, block_size, block_size), values.dtype)], axis=0)


def reference(x_blocks, x_cols, mask_cols, mask_count):
    total_rows = x_blocks.shape[0]
    live_all = jnp.arange(MSLOTS, dtype=jnp.int32)[None, :] < mask_count[:, None]
    group_rows = 32

    def run_product(b_vals, b_cols):
        block_pool = add_empty(b_vals)

        def one_group(begin_row):
            a_vals = lax.dynamic_slice_in_dim(x_blocks, begin_row, group_rows, 0)
            a_cols = lax.dynamic_slice_in_dim(x_cols, begin_row, group_rows, 0)
            out_cols = lax.dynamic_slice_in_dim(mask_cols, begin_row, group_rows, 0)
            live_mask = lax.dynamic_slice_in_dim(live_all, begin_row, group_rows, 0)
            return pick_product(a_vals, a_cols.astype(jnp.int32), block_pool, b_cols, out_cols, live_mask)

        group_starts = jnp.arange(total_rows // group_rows, dtype=jnp.int32) * group_rows
        result = lax.map(one_group, group_starts)
        return result.reshape(total_rows, MSLOTS, BS, BS)

    square = run_product(x_blocks, x_cols)
    x_cubed = run_product(square, mask_cols)
    return square, x_cubed
```

```python
import jax
import jax.numpy as jnp
from jax import lax
from jax.experimental import pallas as pl
from jax.experimental.pallas import tpu as pltpu
from jax.sharding import PartitionSpec as P

GX, GY, GZ = 48, 4, 8
BS = 128
SLOTS = 6

ZERO, UP1, DOWN1, TWO1, UP2, DOWN2, TWO2, UP3 = range(8)
OFFSETS = ((0, 0, 0), (1, 0, 0), (-1, 0, 0), (2, 0, 0), (0, 1, 0), (0, -1, 0), (0, 2, 0), (0, 0, 1))

POS1, POS2, POS3, NPOS1, NPOS2, NPOS3, FPOS2, NEAR2 = range(8)
SLOT_OF = 8
HAS1_ZERO, HAS1_STEP, HAS2_ZERO, HAS2_STEP, HAS2_TWO, HAS3_ZERO, HAS3_STEP = range(16, 23)
META = 24


def wrap(value, size):
    value = jnp.where(value >= size, value - size, value)
    return jnp.where(value < 0, value + size, value)


def structure_kernel(place_ref, xcol_ref, mcol_ref, count_ref, out_ref):
    row, col = place_ref[0], place_ref[1]
    second, third = lax.rem(row, GY), lax.div(row, GY)

    def column(a, b, c):
        return wrap(a, GX) + GX * (wrap(b, GY) + GY * wrap(c, GZ))

    def holds(place, target):
        found = jnp.int32(0)
        count = count_ref[place]
        for m in range(SLOTS):
            hit = jnp.logical_and(count > m, mcol_ref[m, place] == target)
            found = found + hit.astype(jnp.int32)
        return found

    for r in range(2):
        first = 2 * col + r
        me = column(first, second, third)
        pos1 = xcol_ref[1, me] == column(first + 1, second, third)
        pos2 = xcol_ref[2, me] == column(first, second + 1, third)
        pos3 = xcol_ref[3, me] == column(first, second, third + 1)
        s1, s2, s3 = (jnp.where(p, 1, -1) for p in (pos1, pos2, pos3))
        f1, f2, f3 = wrap(first + s1, GX), wrap(second + s2, GY), wrap(third + s3, GZ)
        c1, c2, c3 = column(f1, second, third), column(first, f2, third), column(first, second, f3)
        far2 = column(first, f2 + s2, third)
        npos1 = xcol_ref[1, c1] == column(f1 + 1, second, third)
        npos2 = xcol_ref[2, c2] == column(first, f2 + 1, third)
        npos3 = xcol_ref[3, c3] == column(first, second, f3 + 1)
        fpos2 = xcol_ref[2, far2] == column(first, f2 + s2 + 1 - jnp.where(f2 + s2 >= GY, GY, 0), third)
        even = lax.rem(second, 2) == 0
        for place, flag in (
            (POS1, pos1),
            (POS2, pos2),
            (POS3, pos3),
            (NPOS1, npos1),
            (NPOS2, npos2),
            (NPOS3, npos3),
            (FPOS2, fpos2),
            (NEAR2, pos2 == even),
        ):
            out_ref[r, place] = flag.astype(jnp.int32)
        count = count_ref[me]
        for k, (a, b, c) in enumerate(OFFSETS):
            target = column(first + a, second + b, third + c)
            slot = jnp.int32(-1)
            for m in range(SLOTS):
                hit = jnp.logical_and(count > m, mcol_ref[m, me] == target)
                slot = jnp.where(hit, m, slot)
            out_ref[r, SLOT_OF + k] = slot
        n1, n2 = jnp.where(npos1, 1, -1), jnp.where(npos2, 1, -1)
        out_ref[r, HAS1_ZERO] = holds(c1, c1)
        out_ref[r, HAS1_STEP] = holds(c1, column(f1 + n1, second, third))
        out_ref[r, HAS2_ZERO] = holds(c2, c2)
        out_ref[r, HAS2_STEP] = holds(c2, column(first, f2 + n2, third))
        out_ref[r, HAS2_TWO] = holds(c2, column(first, f2 + 2, third))
        out_ref[r, HAS3_ZERO] = holds(c3, c3)
        out_ref[r, HAS3_STEP] = holds(c3, column(first, second, f3 + 1))
        out_ref[r, META - 1] = jnp.int32(0)


def halves(value):
    high = value.astype(jnp.bfloat16)
    low = (value - high.astype(jnp.float32)).astype(jnp.bfloat16)
    return high, low


def left(value):
    high, low = halves(value)
    return jnp.concatenate([high, low, high], axis=1)


def right(value):
    high, low = halves(value)
    return jnp.concatenate([high, high, low], axis=0)


def product(lefts, rights):
    a = lefts[0] if len(lefts) == 1 else jnp.concatenate(lefts, axis=1)
    b = rights[0] if len(rights) == 1 else jnp.concatenate(rights, axis=0)
    return jnp.dot(a, b, preferred_element_type=jnp.float32)


def row_view(meta, r):
    flag = lambda k: meta[r, k] != 0
    slot = lambda k: meta[r, SLOT_OF + k]
    return flag, slot


def first_neighbour(r, pos1, x, from_left, from_right):
    ups = (x[1, 0], x[1, 1]) if r == 0 else (from_right[0], from_right[1])
    downs = (from_left[0], from_left[1]) if r == 0 else (x[0, 0], x[0, 1])
    return jnp.where(pos1, ups[0], downs[0]), jnp.where(pos1, ups[1], downs[1])


def square_kernel(
    meta, x, from_left, from_right, near, across, above, below, square, middle, middle0, middle1
):
    square[...] = jnp.zeros_like(square)
    for r in range(2):
        flag, slot = row_view(meta, r)
        pos1, pos2, pos3 = flag(POS1), flag(POS2), flag(POS3)
        mutual = [flag(POS1 + k) != flag(NPOS1 + k) for k in range(3)]
        d, a1, a2, a3 = (x[r, s] for s in range(4))
        d1, b1 = first_neighbour(r, pos1, x, from_left, from_right)
        near2 = flag(NEAR2)
        d2 = jnp.where(near2, near[0, r], across[0, r])
        b2 = jnp.where(near2, near[1, r], across[1, r])
        d3 = above[0, r]
        b3 = jnp.where(pos3, above[1, r], below[r])
        ld, l1, l2, l3 = left(d), left(a1), left(a2), left(a3)
        zero = jnp.zeros_like(d)

        centre = product(
            [ld, l1, l2, l3],
            [right(d)] + [right(jnp.where(m, b, zero)) for m, b in zip(mutual, (b1, b2, b3))],
        )
        middle[r] = centre
        (middle0 if r == 0 else middle1)[0] = centre

        @pl.when(slot(ZERO) >= 0)
        def _():
            square[r, slot(ZERO)] = centre

        step1 = jnp.where(pos1, slot(UP1), slot(DOWN1))
        step2 = jnp.where(pos2, slot(UP2), slot(DOWN2))

        @pl.when(step1 >= 0)
        def _():
            square[r, step1] = product([ld, l1], [right(a1), right(d1)])

        @pl.when(jnp.logical_and(slot(TWO1) >= 0, jnp.logical_and(pos1, flag(NPOS1))))
        def _():
            square[r, slot(TWO1)] = product([l1], [right(b1)])

        @pl.when(step2 >= 0)
        def _():
            square[r, step2] = product([ld, l2], [right(a2), right(d2)])

        @pl.when(jnp.logical_and(slot(TWO2) >= 0, pos2 == flag(NPOS2)))
        def _():
            square[r, slot(TWO2)] = product([l2], [right(b2)])

        @pl.when(jnp.logical_and(slot(UP3) >= 0, pos3))
        def _():
            square[r, slot(UP3)] = product([ld, l3], [right(a3), right(d3)])


def cube_kernel(
    meta,
    x,
    square,
    from_left,
    from_right,
    right_next,
    near,
    across,
    opposite,
    above,
    below,
    below_d,
    mid_left,
    mid_right,
    mid_local,
    mid_near,
    mid_across,
    mid_above,
    cube,
):
    for r in range(2):
        flag, slot = row_view(meta, r)
        pos1, pos2, pos3 = flag(POS1), flag(POS2), flag(POS3)
        npos1, npos2 = flag(NPOS1), flag(NPOS2)
        d, a1, a2, a3 = (x[r, s] for s in range(4))
        ld = left(d)
        for m in range(SLOTS):
            cube[r, m] = product([ld], [right(square[r, m])])

        step1 = jnp.where(pos1, slot(UP1), slot(DOWN1))
        mutual1 = pos1 != npos1
        other1 = jnp.where(mutual1, slot(ZERO), jnp.where(pos1, slot(TWO1), -1))
        d1, b1 = first_neighbour(r, pos1, x, from_left, from_right)

        @pl.when(jnp.logical_and(step1 >= 0, flag(HAS1_ZERO)))
        def _():
            up = mid_local[1] if r == 0 else mid_right[0]
            down = mid_left[0] if r == 0 else mid_local[0]
            cube[r, step1] += product([left(a1)], [right(jnp.where(pos1, up, down))])

        @pl.when(jnp.logical_and(other1 >= 0, flag(HAS1_STEP)))
        def _():
            beyond = jnp.where(mutual1, d, from_right[0] if r == 0 else right_next[0])
            step = product([left(d1), left(b1)], [right(b1), right(beyond)])
            cube[r, other1] += product([left(a1)], [right(step)])

        near2 = flag(NEAR2)
        step2 = jnp.where(pos2, slot(UP2), slot(DOWN2))
        back2 = jnp.where(pos2, slot(DOWN2), slot(UP2))
        mutual2 = pos2 != npos2
        other2 = jnp.where(mutual2, slot(ZERO), slot(TWO2))
        d2 = jnp.where(near2, near[0, r], across[0, r])
        b2 = jnp.where(near2, near[1, r], across[1, r])

        @pl.when(jnp.logical_and(step2 >= 0, flag(HAS2_ZERO)))
        def _():
            middle = jnp.where(near2, mid_near[r], mid_across[r])
            cube[r, step2] += product([left(a2)], [right(middle)])

        @pl.when(jnp.logical_and(other2 >= 0, flag(HAS2_STEP)))
        def _():
            beyond = jnp.where(mutual2, d, opposite[0, r])
            step = product([left(d2), left(b2)], [right(b2), right(beyond)])
            cube[r, other2] += product([left(a2)], [right(step)])

        onward2 = jnp.logical_and(jnp.logical_not(mutual2), npos2 == flag(FPOS2))

        @pl.when(jnp.logical_and(onward2, jnp.logical_and(back2 >= 0, flag(HAS2_TWO))))
        def _():
            two = product([left(b2)], [right(opposite[1, r])])
            cube[r, back2] += product([left(a2)], [right(two)])

        @pl.when(jnp.logical_and(pos3, jnp.logical_and(slot(UP3) >= 0, flag(HAS3_ZERO))))
        def _():
            cube[r, slot(UP3)] += product([left(a3)], [right(mid_above[r])])

        back3 = jnp.logical_and(jnp.logical_not(pos3), flag(NPOS3))

        @pl.when(jnp.logical_and(back3, jnp.logical_and(slot(ZERO) >= 0, flag(HAS3_STEP))))
        def _():
            b3 = below[r]
            step = product([left(below_d[r]), left(b3)], [right(b3), right(d)])
            cube[r, slot(ZERO)] += product([left(a3)], [right(step)])


def call(kernel, out_shapes, *operands, smem=0, smem_out=False, flops=0):
    spaces = [pltpu.SMEM] * smem + [pltpu.VMEM] * (len(operands) - smem)
    out_space = pltpu.SMEM if smem_out else pltpu.VMEM
    return pl.pallas_call(
        kernel,
        out_shape=out_shapes,
        in_specs=[pl.BlockSpec(memory_space=s) for s in spaces],
        out_specs=jax.tree.map(lambda _: pl.BlockSpec(memory_space=out_space), out_shapes),
        compiler_params=pltpu.CompilerParams(vmem_limit_bytes=32 * 2**20),
        cost_estimate=pl.CostEstimate(flops=flops, bytes_accessed=2**21, transcendentals=0),
    )(*operands)


def per_device(x, x_cols, mask_cols, mask_count):
    row_count, col_count = lax.axis_size("row"), lax.axis_size("col")
    row, col = lax.axis_index("row"), lax.axis_index("col")

    def along(value, axis, target, count):
        return lax.ppermute(value, axis, [(i, target(i) % count) for i in range(count)])

    def to_col(value, step):
        return along(value, "col", lambda i: i + step, col_count)

    def to_row(value, step):
        return along(value, "row", lambda i: i + step, row_count)

    def flip_row(value, bits):
        return along(value, "row", lambda i: i ^ bits, row_count)

    block = lambda *lead: jax.ShapeDtypeStruct(lead + (BS, BS), jnp.float32)

    pair2 = jnp.stack([x[:, 0], x[:, 2]])
    pair3 = jnp.stack([x[:, 0], x[:, 3]])
    above = to_row(pair3, -GY)
    below = to_row(x[:, 3], GY)
    opposite = flip_row(pair2, 2)
    near = flip_row(pair2, 1)
    from_left = to_col(x[1, 0:2], 1)
    from_right = to_col(x[0, 0:2], -1)
    across = flip_row(opposite, 1)
    below_d = to_row(x[:, 0], GY)
    right_next = to_col(x[1, 0:1], -1)

    place = jnp.stack([row, col]).astype(jnp.int32)
    meta = call(
        structure_kernel,
        jax.ShapeDtypeStruct((2, META), jnp.int32),
        place,
        x_cols.T,
        mask_cols.T,
        mask_count,
        smem=4,
        smem_out=True,
    )
    square, middle, middle0, middle1 = call(
        square_kernel,
        [block(2, SLOTS), block(2), block(1), block(1)],
        meta,
        x,
        from_left,
        from_right,
        near,
        across,
        above,
        below,
        smem=1,
        flops=60 * 2 * BS**3,
    )
    mid_above = to_row(middle, -GY)
    mid_left = to_col(middle1, 1)
    mid_right = to_col(middle0, -1)
    mid_across = flip_row(middle, 3)
    mid_near = flip_row(middle, 1)
    cube = call(
        cube_kernel,
        block(2, SLOTS),
        meta,
        x,
        square,
        from_left,
        from_right,
        right_next,
        near,
        across,
        opposite,
        above,
        below,
        below_d,
        mid_left,
        mid_right,
        middle,
        mid_near,
        mid_across,
        mid_above,
        smem=1,
        flops=80 * 2 * BS**3,
    )
    return square, cube


def solution(mesh):
    in_specs = (P(("row", "col"), None, None, None), P(), P(), P())
    out_specs = (P(("row", "col"), None, None, None), P(("row", "col"), None, None, None))
    return jax.shard_map(
        per_device, mesh=mesh, in_specs=in_specs, out_specs=out_specs, check_vma=False
    )
```

```python
import jax
import jax.numpy as jnp
from jax import lax
from jax.experimental import pallas as pl
from jax.experimental.pallas import tpu as pltpu
from jax.sharding import PartitionSpec as P

GX, GY, GZ = 48, 4, 8
BS = 128
SLOTS = 6

ZERO, UP1, DOWN1, TWO1, UP2, DOWN2, TWO2, UP3 = range(8)
OFFSETS = ((0, 0, 0), (1, 0, 0), (-1, 0, 0), (2, 0, 0), (0, 1, 0), (0, -1, 0), (0, 2, 0), (0, 0, 1))

POS1, POS2, POS3, NPOS1, NPOS2, NPOS3, FPOS2, NEAR2 = range(8)
SLOT_OF = 8
HAS1_ZERO, HAS1_STEP, HAS2_ZERO, HAS2_STEP, HAS2_TWO, HAS3_ZERO, HAS3_STEP, RELAY_OWN = range(16, 24)
META = 24


def wrap(value, size):
    value = jnp.where(value >= size, value - size, value)
    return jnp.where(value < 0, value + size, value)


def structure_kernel(place_ref, xcol_ref, mcol_ref, count_ref, out_ref):
    row, col = place_ref[0], place_ref[1]
    second, third = lax.rem(row, GY), lax.div(row, GY)

    def column(a, b, c):
        return wrap(a, GX) + GX * (wrap(b, GY) + GY * wrap(c, GZ))

    def holds(place, target):
        found = jnp.int32(0)
        count = count_ref[place]
        for m in range(SLOTS):
            hit = jnp.logical_and(count > m, mcol_ref[m, place] == target)
            found = found + hit.astype(jnp.int32)
        return found

    for r in range(2):
        first = 2 * col + r
        me = column(first, second, third)
        pos1 = xcol_ref[1, me] == column(first + 1, second, third)
        pos2 = xcol_ref[2, me] == column(first, second + 1, third)
        pos3 = xcol_ref[3, me] == column(first, second, third + 1)
        s1, s2, s3 = (jnp.where(p, 1, -1) for p in (pos1, pos2, pos3))
        f1, f2, f3 = wrap(first + s1, GX), wrap(second + s2, GY), wrap(third + s3, GZ)
        c1, c2, c3 = column(f1, second, third), column(first, f2, third), column(first, second, f3)
        far2 = column(first, f2 + s2, third)
        npos1 = xcol_ref[1, c1] == column(f1 + 1, second, third)
        npos2 = xcol_ref[2, c2] == column(first, f2 + 1, third)
        npos3 = xcol_ref[3, c3] == column(first, second, f3 + 1)
        fpos2 = xcol_ref[2, far2] == column(first, f2 + s2 + 1 - jnp.where(f2 + s2 >= GY, GY, 0), third)
        even = lax.rem(second, 2) == 0
        for place, flag in (
            (POS1, pos1),
            (POS2, pos2),
            (POS3, pos3),
            (NPOS1, npos1),
            (NPOS2, npos2),
            (NPOS3, npos3),
            (FPOS2, fpos2),
            (NEAR2, pos2 == even),
        ):
            out_ref[r, place] = flag.astype(jnp.int32)
        count = count_ref[me]
        for k, (a, b, c) in enumerate(OFFSETS):
            target = column(first + a, second + b, third + c)
            slot = jnp.int32(-1)
            for m in range(SLOTS):
                hit = jnp.logical_and(count > m, mcol_ref[m, me] == target)
                slot = jnp.where(hit, m, slot)
            out_ref[r, SLOT_OF + k] = slot
        n1, n2 = jnp.where(npos1, 1, -1), jnp.where(npos2, 1, -1)
        out_ref[r, HAS1_ZERO] = holds(c1, c1)
        out_ref[r, HAS1_STEP] = holds(c1, column(f1 + n1, second, third))
        out_ref[r, HAS2_ZERO] = holds(c2, c2)
        out_ref[r, HAS2_STEP] = holds(c2, column(first, f2 + n2, third))
        out_ref[r, HAS2_TWO] = holds(c2, column(first, f2 + 2, third))
        out_ref[r, HAS3_ZERO] = holds(c3, c3)
        out_ref[r, HAS3_STEP] = holds(c3, column(first, second, f3 + 1))
        odd = lax.rem(third, 2)
        partner = third + 1 - 2 * odd
        wants_up = xcol_ref[3, column(first, second, partner)] == column(first, second, partner + 1)
        out_ref[r, RELAY_OWN] = (wants_up == (odd == 1)).astype(jnp.int32)


def halves(value):
    high = value.astype(jnp.bfloat16)
    low = (value - high.astype(jnp.float32)).astype(jnp.bfloat16)
    return high, low


def left(value):
    high, low = halves(value)
    return jnp.concatenate([high, low, high], axis=1)


def right(value):
    high, low = halves(value)
    return jnp.concatenate([high, high, low], axis=0)


def product(lefts, rights):
    a = lefts[0] if len(lefts) == 1 else jnp.concatenate(lefts, axis=1)
    b = rights[0] if len(rights) == 1 else jnp.concatenate(rights, axis=0)
    return jnp.dot(a, b, preferred_element_type=jnp.float32)


def row_view(meta, r):
    flag = lambda k: meta[r, k] != 0
    slot = lambda k: meta[r, SLOT_OF + k]
    return flag, slot


def first_neighbour(r, pos1, x, from_left, from_right):
    ups = (x[1, 0], x[1, 1]) if r == 0 else (from_right[0], from_right[1])
    downs = (from_left[0], from_left[1]) if r == 0 else (x[0, 0], x[0, 1])
    return jnp.where(pos1, ups[0], downs[0]), jnp.where(pos1, ups[1], downs[1])


def second_neighbour(r, near2, near, across):
    return jnp.where(near2, near[0, r], across[0, r]), jnp.where(near2, near[1, r], across[1, r])


def middle_kernel(meta, x, from_left, from_right, near, across, third, middle, middle0, middle1):
    for r in range(2):
        flag, _ = row_view(meta, r)
        d, a1, a2, a3 = (x[r, s] for s in range(4))
        _, b1 = first_neighbour(r, flag(POS1), x, from_left, from_right)
        _, b2 = second_neighbour(r, flag(NEAR2), near, across)
        b3 = third[1, r]
        zero = jnp.zeros_like(d)
        mutual = [flag(POS1 + k) != flag(NPOS1 + k) for k in range(3)]
        centre = product(
            [left(d), left(a1), left(a2), left(a3)],
            [right(d)] + [right(jnp.where(m, b, zero)) for m, b in zip(mutual, (b1, b2, b3))],
        )
        middle[r] = centre
        (middle0 if r == 0 else middle1)[0] = centre


def square_kernel(
    meta, x, middle, from_left, from_right, near, across, opposite, third, square, cube
):
    square[...] = jnp.zeros_like(square)
    for r in range(2):
        flag, slot = row_view(meta, r)
        pos1, pos2, pos3 = flag(POS1), flag(POS2), flag(POS3)
        npos1, npos2, npos3 = flag(NPOS1), flag(NPOS2), flag(NPOS3)
        d, a1, a2, a3 = (x[r, s] for s in range(4))
        d1, b1 = first_neighbour(r, pos1, x, from_left, from_right)
        d2, b2 = second_neighbour(r, flag(NEAR2), near, across)
        d3, b3 = third[0, r], third[1, r]
        ld, l1, l2, l3 = left(d), left(a1), left(a2), left(a3)

        @pl.when(slot(ZERO) >= 0)
        def _():
            square[r, slot(ZERO)] = middle[r]

        step1 = jnp.where(pos1, slot(UP1), slot(DOWN1))
        step2 = jnp.where(pos2, slot(UP2), slot(DOWN2))

        @pl.when(step1 >= 0)
        def _():
            square[r, step1] = product([ld, l1], [right(a1), right(d1)])

        @pl.when(jnp.logical_and(slot(TWO1) >= 0, jnp.logical_and(pos1, npos1)))
        def _():
            square[r, slot(TWO1)] = product([l1], [right(b1)])

        @pl.when(step2 >= 0)
        def _():
            square[r, step2] = product([ld, l2], [right(a2), right(d2)])

        @pl.when(jnp.logical_and(slot(TWO2) >= 0, pos2 == npos2))
        def _():
            square[r, slot(TWO2)] = product([l2], [right(b2)])

        @pl.when(jnp.logical_and(slot(UP3) >= 0, pos3))
        def _():
            square[r, slot(UP3)] = product([ld, l3], [right(a3), right(d3)])

        for m in range(SLOTS):
            cube[r, m] = product([ld], [right(square[r, m])])

        mutual1 = pos1 != npos1
        other1 = jnp.where(mutual1, slot(ZERO), jnp.where(pos1, slot(TWO1), -1))

        @pl.when(jnp.logical_and(other1 >= 0, flag(HAS1_STEP)))
        def _():
            beyond = jnp.where(mutual1, d, from_right[2 * r])
            step = product([left(d1), left(b1)], [right(b1), right(beyond)])
            cube[r, other1] += product([l1], [right(step)])

        mutual2 = pos2 != npos2
        other2 = jnp.where(mutual2, slot(ZERO), slot(TWO2))
        back2 = jnp.where(pos2, slot(DOWN2), slot(UP2))

        @pl.when(jnp.logical_and(other2 >= 0, flag(HAS2_STEP)))
        def _():
            beyond = jnp.where(mutual2, d, opposite[0, r])
            step = product([left(d2), left(b2)], [right(b2), right(beyond)])
            cube[r, other2] += product([l2], [right(step)])

        onward2 = jnp.logical_and(jnp.logical_not(mutual2), npos2 == flag(FPOS2))

        @pl.when(jnp.logical_and(onward2, jnp.logical_and(back2 >= 0, flag(HAS2_TWO))))
        def _():
            two = product([left(b2)], [right(opposite[1, r])])
            cube[r, back2] += product([l2], [right(two)])

        back3 = jnp.logical_and(jnp.logical_not(pos3), npos3)

        @pl.when(jnp.logical_and(back3, jnp.logical_and(slot(ZERO) >= 0, flag(HAS3_STEP))))
        def _():
            step = product([left(d3), left(b3)], [right(b3), right(d)])
            cube[r, slot(ZERO)] += product([l3], [right(step)])


def cube_kernel(meta, x, part, middle, mid_left, mid_right, mid_near, mid_across, mid_above, cube):
    cube[...] = part[...]
    for r in range(2):
        flag, slot = row_view(meta, r)
        pos1, pos2, pos3 = flag(POS1), flag(POS2), flag(POS3)
        step1 = jnp.where(pos1, slot(UP1), slot(DOWN1))
        step2 = jnp.where(pos2, slot(UP2), slot(DOWN2))

        @pl.when(jnp.logical_and(step1 >= 0, flag(HAS1_ZERO)))
        def _():
            up = middle[1] if r == 0 else mid_right[0]
            down = mid_left[0] if r == 0 else middle[0]
            cube[r, step1] += product([left(x[r, 1])], [right(jnp.where(pos1, up, down))])

        @pl.when(jnp.logical_and(step2 >= 0, flag(HAS2_ZERO)))
        def _():
            beside = jnp.where(flag(NEAR2), mid_near[r], mid_across[r])
            cube[r, step2] += product([left(x[r, 2])], [right(beside)])

        @pl.when(jnp.logical_and(pos3, jnp.logical_and(slot(UP3) >= 0, flag(HAS3_ZERO))))
        def _():
            cube[r, slot(UP3)] += product([left(x[r, 3])], [right(mid_above[r])])


def call(kernel, out_shapes, *operands, smem=0, smem_out=False, flops=0):
    spaces = [pltpu.SMEM] * smem + [pltpu.VMEM] * (len(operands) - smem)
    out_space = pltpu.SMEM if smem_out else pltpu.VMEM
    return pl.pallas_call(
        kernel,
        out_shape=out_shapes,
        in_specs=[pl.BlockSpec(memory_space=s) for s in spaces],
        out_specs=jax.tree.map(lambda _: pl.BlockSpec(memory_space=out_space), out_shapes),
        compiler_params=pltpu.CompilerParams(vmem_limit_bytes=32 * 2**20),
        cost_estimate=pl.CostEstimate(flops=flops, bytes_accessed=2**21, transcendentals=0),
    )(*operands)


def per_device(x, x_cols, mask_cols, mask_count):
    row_count, col_count = lax.axis_size("row"), lax.axis_size("col")
    row, col = lax.axis_index("row"), lax.axis_index("col")

    def along(value, axis, target, count):
        return lax.ppermute(value, axis, [(i, target(i) % count) for i in range(count)])

    def to_col(value, step):
        return along(value, "col", lambda i: i + step, col_count)

    def to_row(value, step):
        return along(value, "row", lambda i: i + step, row_count)

    def flip_row(value, bits):
        return along(value, "row", lambda i: i ^ bits, row_count)

    block = lambda *lead: jax.ShapeDtypeStruct(lead + (BS, BS), jnp.float32)

    pair2 = jnp.stack([x[:, 0], x[:, 2]])
    pair3 = jnp.stack([x[:, 0], x[:, 3]])
    relayed = along(pair3, "row", lambda i: i + 2 * GY * (2 * (i // GY % 2) - 1), row_count)
    from_right = to_col(jnp.stack([x[0, 0], x[0, 1], x[1, 0]]), -1)
    from_left = to_col(x[1, 0:2], 1)
    opposite = flip_row(pair2, 2)
    near = flip_row(pair2, 1)

    place = jnp.stack([row, col]).astype(jnp.int32)
    meta = call(
        structure_kernel,
        jax.ShapeDtypeStruct((2, META), jnp.int32),
        place,
        x_cols.T,
        mask_cols.T,
        mask_count,
        smem=4,
        smem_out=True,
    )
    own = meta[:, RELAY_OWN][None, :, None, None] != 0
    third = flip_row(jnp.where(own, pair3, relayed), GY)
    across = flip_row(opposite, 1)
    middle, middle0, middle1 = call(
        middle_kernel,
        [block(2), block(1), block(1)],
        meta,
        x,
        from_left,
        from_right,
        near,
        across,
        third,
        smem=1,
        flops=24 * 2 * BS**3,
    )
    mid_above = to_row(middle, -GY)
    mid_left = to_col(middle1, 1)
    mid_right = to_col(middle0, -1)
    mid_across = flip_row(middle, 3)
    mid_near = flip_row(middle, 1)
    square, part = call(
        square_kernel,
        [block(2, SLOTS), block(2, SLOTS)],
        meta,
        x,
        middle,
        from_left,
        from_right,
        near,
        across,
        opposite,
        third,
        smem=1,
        flops=100 * 2 * BS**3,
    )
    cube = call(
        cube_kernel,
        block(2, SLOTS),
        meta,
        x,
        part,
        middle,
        mid_left,
        mid_right,
        mid_near,
        mid_across,
        mid_above,
        smem=1,
        flops=18 * 2 * BS**3,
    )
    return square, cube


def solution(mesh):
    in_specs = (P(("row", "col"), None, None, None), P(), P(), P())
    out_specs = (P(("row", "col"), None, None, None), P(("row", "col"), None, None, None))
    return jax.shard_map(
        per_device, mesh=mesh, in_specs=in_specs, out_specs=out_specs, check_vma=False
    )
```

```python
import jax
import jax.numpy as jnp
from jax import lax
from jax.experimental import pallas as pl
from jax.experimental.pallas import tpu as pltpu
from jax.sharding import PartitionSpec as P

GX, GY, GZ = 48, 4, 8
BS = 128
SLOTS = 6
FIRST_FLOPS = 10**10
RING = 8

ZERO, UP1, DOWN1, TWO1, UP2, DOWN2, TWO2, UP3 = range(8)
OFFSETS = ((0, 0, 0), (1, 0, 0), (-1, 0, 0), (2, 0, 0), (0, 1, 0), (0, -1, 0), (0, 2, 0), (0, 0, 1))

POS1, POS2, POS3, NPOS1, NPOS2, NPOS3, FPOS2, NEAR2 = range(8)
SLOT_OF = 8
HAS1_ZERO, HAS1_STEP, HAS2_ZERO, HAS2_STEP, HAS2_TWO, HAS3_ZERO, HAS3_STEP = range(16, 23)
FIX_LEFT, FIX_RIGHT, OTHER = 23, 24, 25
META = 26


def wrap(value, size):
    value = jnp.where(value >= size, value - size, value)
    return jnp.where(value < 0, value + size, value)


def structure_kernel(place_ref, xcol_ref, mcol_ref, count_ref, out_ref):
    row, col = place_ref[0], place_ref[1]
    second, third = lax.rem(row, GY), lax.div(row, GY)

    def column(a, b, c):
        return wrap(a, GX) + GX * (wrap(b, GY) + GY * wrap(c, GZ))

    def holds(place, target):
        found = jnp.int32(0)
        count = count_ref[place]
        for m in range(SLOTS):
            hit = jnp.logical_and(count > m, mcol_ref[m, place] == target)
            found = found + hit.astype(jnp.int32)
        return found

    for r in range(2):
        first = 2 * col + r
        me = column(first, second, third)
        pos1 = xcol_ref[1, me] == column(first + 1, second, third)
        pos2 = xcol_ref[2, me] == column(first, second + 1, third)
        pos3 = xcol_ref[3, me] == column(first, second, third + 1)
        s1, s2, s3 = (jnp.where(p, 1, -1) for p in (pos1, pos2, pos3))
        f1, f2, f3 = wrap(first + s1, GX), wrap(second + s2, GY), wrap(third + s3, GZ)
        c1, c2, c3 = column(f1, second, third), column(first, f2, third), column(first, second, f3)
        far2 = column(first, f2 + s2, third)
        npos1 = xcol_ref[1, c1] == column(f1 + 1, second, third)
        npos2 = xcol_ref[2, c2] == column(first, f2 + 1, third)
        npos3 = xcol_ref[3, c3] == column(first, second, f3 + 1)
        fpos2 = xcol_ref[2, far2] == column(first, f2 + s2 + 1 - jnp.where(f2 + s2 >= GY, GY, 0), third)
        even = lax.rem(second, 2) == 0
        for place, flag in (
            (POS1, pos1),
            (POS2, pos2),
            (POS3, pos3),
            (NPOS1, npos1),
            (NPOS2, npos2),
            (NPOS3, npos3),
            (FPOS2, fpos2),
            (NEAR2, pos2 == even),
        ):
            out_ref[r, place] = flag.astype(jnp.int32)
        count = count_ref[me]
        for k, (a, b, c) in enumerate(OFFSETS):
            target = column(first + a, second + b, third + c)
            slot = jnp.int32(-1)
            for m in range(SLOTS):
                hit = jnp.logical_and(count > m, mcol_ref[m, me] == target)
                slot = jnp.where(hit, m, slot)
            out_ref[r, SLOT_OF + k] = slot
        n1, n2 = jnp.where(npos1, 1, -1), jnp.where(npos2, 1, -1)
        out_ref[r, HAS1_ZERO] = holds(c1, c1)
        out_ref[r, HAS1_STEP] = holds(c1, column(f1 + n1, second, third))
        out_ref[r, HAS2_ZERO] = holds(c2, c2)
        out_ref[r, HAS2_STEP] = holds(c2, column(first, f2 + n2, third))
        out_ref[r, HAS2_TWO] = holds(c2, column(first, f2 + 2, third))
        out_ref[r, HAS3_ZERO] = holds(c3, c3)
        out_ref[r, HAS3_STEP] = holds(c3, column(first, second, f3 + 1))
        out_ref[r, OTHER] = 1 - lax.rem(row, 2)
        out_ref[r, FIX_LEFT] = (lax.rem(col, RING) == 0).astype(jnp.int32)
        out_ref[r, FIX_RIGHT] = (lax.rem(col, RING) == RING - 1).astype(jnp.int32)


def halves(value):
    high = value.astype(jnp.bfloat16)
    low = (value - high.astype(jnp.float32)).astype(jnp.bfloat16)
    return high, low


def left(value):
    high, low = halves(value)
    return jnp.concatenate([high, low, high], axis=1)


def right(value):
    high, low = halves(value)
    return jnp.concatenate([high, high, low], axis=0)


def product(lefts, rights):
    a = lefts[0] if len(lefts) == 1 else jnp.concatenate(lefts, axis=1)
    b = rights[0] if len(rights) == 1 else jnp.concatenate(rights, axis=0)
    return jnp.dot(a, b, preferred_element_type=jnp.float32)


def row_view(meta, r):
    flag = lambda k: meta[r, k] != 0
    slot = lambda k: meta[r, SLOT_OF + k]
    return flag, slot


def from_side(flag, fix, ring, wraps, k):
    return jnp.where(flag(fix), wraps[k // 2][k % 2], ring[k])


def first_neighbour(r, flag, x, ring_left, ring_right, wraps):
    blocks = []
    for k in range(2):
        up = x[1, k] if r == 0 else from_side(flag, FIX_RIGHT, ring_right, wraps, k)
        down = from_side(flag, FIX_LEFT, ring_left, wraps, k) if r == 0 else x[0, k]
        blocks.append(jnp.where(flag(POS1), up, down))
    return blocks


def second_neighbour(meta, r, flag, near, across):
    other = meta[0, OTHER]
    return [jnp.where(flag(NEAR2), near[other, k, r], across[k, r]) for k in range(2)]


def base_kernel(
    meta, x, near, across, above, below, base, sides, third, to_left, to_right, to_wrap
):
    to_left[0:2] = x[0, 0:2]
    to_left[3] = x[1, 0]
    to_right[0:2] = x[1, 0:2]
    to_wrap[1] = x[1, 0]
    inside = jnp.logical_and(meta[0, POS1] != 0, meta[1, POS1] == 0)
    for r in range(2):
        flag, _ = row_view(meta, r)
        d, a1, a2, a3 = (x[r, s] for s in range(4))
        d2, b2 = second_neighbour(meta, r, flag, near, across)
        b3 = jnp.where(flag(POS3), above[r], below[r])
        third[r] = b3
        rights = [right(x[1 - r, 1]), right(b2), right(b3)]
        mutual = [inside] + [flag(POS1 + k) != flag(NPOS1 + k) for k in (1, 2)]
        none = jnp.zeros_like(rights[0])
        ld, l2 = left(d), left(a2)
        sides[0, r] = product([ld, l2], [right(a2), right(d2)])
        sides[1, r] = product([l2], [rights[1]])
        value = product(
            [ld, left(a1), l2, left(a3)],
            [right(d)] + [jnp.where(m, b, none) for m, b in zip(mutual, rights)],
        )
        base[r] = value
        (to_left if r == 0 else to_right)[2] = value
        if r == 0:
            to_wrap[0] = value
        else:

            @pl.when(flag(FIX_RIGHT))
            def _():
                to_wrap[0] = value


def early_kernel(meta, x, sides, square, cube):
    square[...] = jnp.zeros_like(square)
    cube[...] = jnp.zeros_like(cube)
    for r in range(2):
        flag, slot = row_view(meta, r)
        ld = left(x[r, 0])
        step2 = jnp.where(flag(POS2), slot(UP2), slot(DOWN2))
        twice2 = jnp.where(flag(POS2) == flag(NPOS2), slot(TWO2), -1)
        for k, where in enumerate((step2, twice2)):

            @pl.when(where >= 0)
            def _():
                square[r, where] = sides[k, r]
                cube[r, where] = product([ld], [right(sides[k, r])])


def copy_kernel(given, taken):
    taken[...] = given[...]


def meeting(flag, r):
    away = flag(POS1) if r == 1 else jnp.logical_not(flag(POS1))
    return away, jnp.logical_and(away, flag(POS1) != flag(NPOS1))


def side_block(flag, r, ring_left, ring_right, wraps, k):
    fix, ring = (FIX_LEFT, ring_left) if r == 0 else (FIX_RIGHT, ring_right)
    return from_side(flag, fix, ring, wraps, k)


def middle_kernel(meta, x, base, sides, ring_left, ring_right, wrap_a, middle, beside, upward):
    beside[1:3] = sides[...]
    for r in range(2):
        flag, _ = row_view(meta, r)
        _, met = meeting(flag, r)
        b1 = side_block(flag, r, ring_left, ring_right, (wrap_a,), 1)
        added = product([left(x[r, 1])], [right(b1)])
        whole = base[r] + jnp.where(met, added, jnp.zeros_like(added))
        middle[r] = whole
        beside[0, r] = whole
        upward[0, r] = whole
        upward[1, r] = x[r, 0]


def late_kernel(
    meta,
    x,
    early,
    early_part,
    middle,
    ring_left,
    ring_right,
    wrap_a,
    third,
    below_d,
    square,
    cube,
):
    wraps = (wrap_a,)
    square[...] = early[...]
    cube[...] = early_part[...]
    for r in range(2):
        flag, slot = row_view(meta, r)
        pos1, pos3, npos1 = flag(POS1), flag(POS3), flag(NPOS1)
        d, a1 = x[r, 0], x[r, 1]
        d1, b1 = first_neighbour(r, flag, x, ring_left, ring_right, wraps)
        ld, l1, r1 = left(d), left(a1), right(b1)

        def put(where, value):
            square[r, where] = value
            cube[r, where] += product([ld], [right(value)])

        step1 = jnp.where(pos1, slot(UP1), slot(DOWN1))

        @pl.when(slot(ZERO) >= 0)
        def _():
            put(slot(ZERO), middle[r])

        @pl.when(step1 >= 0)
        def _():
            put(step1, product([ld, l1], [right(a1), right(d1)]))

        @pl.when(jnp.logical_and(slot(TWO1) >= 0, jnp.logical_and(pos1, npos1)))
        def _():
            put(slot(TWO1), product([l1], [r1]))

        back3 = jnp.logical_and(jnp.logical_not(pos3), flag(NPOS3))

        @pl.when(jnp.logical_and(back3, jnp.logical_and(slot(ZERO) >= 0, flag(HAS3_STEP))))
        def _():
            b3 = third[r]
            step = product([left(below_d[r]), left(b3)], [right(b3), right(d)])
            cube[r, slot(ZERO)] += product([left(x[r, 3])], [right(step)])


def cube_kernel(
    meta,
    x,
    late,
    late_part,
    middle,
    ring_left,
    ring_right,
    wrap_a,
    wrap_b,
    mid_near,
    mid_across,
    mid_above,
    square,
    cube,
):
    wraps = (wrap_a, wrap_b)
    square[...] = late[...]
    cube[...] = late_part[...]
    for r in range(2):
        flag, slot = row_view(meta, r)
        pos1, npos1 = flag(POS1), flag(NPOS1)
        d, a1 = x[r, 0], x[r, 1]
        d1, b1 = first_neighbour(r, flag, x, ring_left, ring_right, wraps)
        l1, r1 = left(a1), right(b1)
        step1 = jnp.where(pos1, slot(UP1), slot(DOWN1))
        step2 = jnp.where(flag(POS2), slot(UP2), slot(DOWN2))
        mutual1 = pos1 != npos1
        other1 = jnp.where(mutual1, slot(ZERO), jnp.where(pos1, slot(TWO1), -1))

        @pl.when(jnp.logical_and(step1 >= 0, flag(HAS1_ZERO)))
        def _():
            away, met = meeting(flag, r)
            back = product([left(b1)], [right(a1)])
            outer = side_block(flag, r, ring_left, ring_right, wraps, 2)
            outer += jnp.where(met, back, jnp.zeros_like(back))
            cube[r, step1] += product([l1], [right(jnp.where(away, outer, middle[1 - r]))])

        @pl.when(jnp.logical_and(other1 >= 0, flag(HAS1_STEP)))
        def _():
            far = from_side(flag, FIX_RIGHT, ring_right, wraps, 3 * r)
            beyond = jnp.where(mutual1, d, far)
            step = product([left(d1), left(b1)], [r1, right(beyond)])
            cube[r, other1] += product([l1], [right(step)])

        pos2, npos2 = flag(POS2), flag(NPOS2)
        back2 = jnp.where(pos2, slot(DOWN2), slot(UP2))
        mutual2 = pos2 != npos2
        other2 = jnp.where(mutual2, slot(ZERO), slot(TWO2))
        onward2 = jnp.where(npos2 == flag(FPOS2), jnp.where(mutual2, -1, back2), -1)
        l2 = left(x[r, 2])
        for k, where, has in (
            (0, step2, HAS2_ZERO),
            (1, other2, HAS2_STEP),
            (2, onward2, HAS2_TWO),
        ):

            @pl.when(jnp.logical_and(where >= 0, flag(has)))
            def _():
                value = jnp.where(flag(NEAR2), mid_near[meta[0, OTHER], k, r], mid_across[k, r])
                cube[r, where] += product([l2], [right(value)])

        @pl.when(jnp.logical_and(slot(UP3) >= 0, flag(POS3)))
        def _():
            a3 = x[r, 3]
            ld, l3 = left(d), left(a3)
            value = product([ld, l3], [right(a3), right(mid_above[1, r])])
            square[r, slot(UP3)] = value
            centre = right(mid_above[0, r])
            centre = jnp.where(flag(HAS3_ZERO), centre, jnp.zeros_like(centre))
            cube[r, slot(UP3)] += product([ld, l3], [right(value), centre])


def call(kernel, out_shapes, *operands, smem=0, free=0, smem_out=False, flops=0):
    held = len(operands) - smem - free
    spaces = [pltpu.SMEM] * smem + [pltpu.VMEM] * held + [pl.ANY] * free
    out_space = pltpu.SMEM if smem_out else pltpu.VMEM
    return pl.pallas_call(
        kernel,
        out_shape=out_shapes,
        in_specs=[pl.BlockSpec(memory_space=s) for s in spaces],
        out_specs=jax.tree.map(lambda _: pl.BlockSpec(memory_space=out_space), out_shapes),
        compiler_params=pltpu.CompilerParams(vmem_limit_bytes=32 * 2**20),
        cost_estimate=pl.CostEstimate(flops=flops, bytes_accessed=2**21, transcendentals=0),
    )(*operands)


def per_device(x, x_cols, mask_cols, mask_count):
    row_count, col_count = lax.axis_size("row"), lax.axis_size("col")
    row, col = lax.axis_index("row"), lax.axis_index("col")

    def along(value, axis, target, count):
        return lax.ppermute(value, axis, [(i, target(i) % count) for i in range(count)])

    def anywhere(value, target):
        pairs = []
        for i in range(row_count * col_count):
            there = target(i // col_count, i % col_count)
            if there is not None:
                pairs.append((i, there[0] * col_count + there[1] % col_count))
        return lax.ppermute(value, ("row", "col"), pairs)

    def to_col(value, step):
        def target(i, j):
            return (i, j + step) if j // RING == (j + step) // RING else None

        return anywhere(value, target)

    def to_wrap(value):
        return anywhere(value, lambda i, j: {0: (i, j - 1), RING - 1: (i, j + 1)}.get(j % RING))

    def to_row(value, step):
        return along(value, "row", lambda i: i + step, row_count)

    def flip_row(value, bits):
        return along(value, "row", lambda i: i ^ bits, row_count)

    def both_cores(value):
        groups = [[i, i + 1] for i in range(0, row_count, 2)]
        return lax.all_gather(value, "row", axis_index_groups=groups)

    block = lambda *lead: jax.ShapeDtypeStruct(lead + (BS, BS), jnp.float32)

    place = jnp.stack([row, col]).astype(jnp.int32)
    pair2 = jnp.stack([x[:, 0], x[:, 2]])
    above = to_row(x[:, 3], -GY)
    below = to_row(x[:, 3], GY)
    below_d = to_row(x[:, 0], GY)
    across = flip_row(pair2, 3)
    edge = lax.dynamic_index_in_dim(x, (lax.rem(col, RING) == RING - 1).astype(jnp.int32), 0, False)
    wrap_a = call(copy_kernel, block(2), to_wrap(edge[0:2]), flops=FIRST_FLOPS)
    near = both_cores(pair2)

    meta = call(
        structure_kernel,
        jax.ShapeDtypeStruct((2, META), jnp.int32),
        *(place, x_cols.T, mask_cols.T, mask_count),
        smem=4,
        smem_out=True,
    )
    base, sides, third, left_message, right_message, wrap_message = call(
        base_kernel,
        [block(2), block(2, 2), block(2), block(4), block(3), block(2)],
        *(meta, x, near, across, above, below),
        smem=1,
        flops=24 * 2 * BS**3,
    )
    ring_right = to_col(left_message, -1)
    ring_left = to_col(right_message, 1)
    wrap_b = call(copy_kernel, block(2), to_wrap(wrap_message), flops=FIRST_FLOPS)
    early, early_part = call(
        early_kernel,
        [block(2, SLOTS), block(2, SLOTS)],
        *(meta, x, sides),
        smem=1,
        flops=12 * 2 * BS**3,
    )
    middle, beside, upward = call(
        middle_kernel,
        [block(2), block(3, 2), block(2, 2)],
        *(meta, x, base, sides, ring_left, ring_right, wrap_a),
        smem=1,
        flops=6 * 2 * BS**3,
    )
    mid_above = to_row(upward, -GY)
    mid_across = flip_row(beside, 3)
    mid_near = both_cores(beside)
    late, late_part = call(
        late_kernel,
        [block(2, SLOTS), block(2, SLOTS)],
        *(meta, x, early, early_part, middle, ring_left, ring_right, wrap_a, third, below_d),
        smem=1,
        flops=50 * 2 * BS**3,
    )
    return call(
        cube_kernel,
        [block(2, SLOTS), block(2, SLOTS)],
        *(meta, x, late, late_part, middle, ring_left, ring_right, wrap_a, wrap_b),
        *(mid_near, mid_across, mid_above),
        smem=1,
        flops=50 * 2 * BS**3,
    )


def solution(mesh):
    in_specs = (P(("row", "col"), None, None, None), P(), P(), P())
    out_specs = (P(("row", "col"), None, None, None), P(("row", "col"), None, None, None))
    return jax.shard_map(
        per_device, mesh=mesh, in_specs=in_specs, out_specs=out_specs, check_vma=False
    )
```

```python
import jax
import jax.numpy as jnp
from jax import lax
from jax.experimental import pallas as pl
from jax.experimental.pallas import tpu as pltpu
from jax.sharding import PartitionSpec as P

GX, GY, GZ = 48, 4, 8
BS = 128
SLOTS = 6
FIRST_FLOPS = 24 * 10**8
RING = 8

ZERO, UP1, DOWN1, TWO1, UP2, DOWN2, TWO2, UP3 = range(8)
OFFSETS = ((0, 0, 0), (1, 0, 0), (-1, 0, 0), (2, 0, 0), (0, 1, 0), (0, -1, 0), (0, 2, 0), (0, 0, 1))

POS1, POS2, POS3, NPOS1, NPOS2, NPOS3, FPOS2, NEAR2 = range(8)
SLOT_OF = 8
HAS1_ZERO, HAS1_STEP, HAS2_ZERO, HAS2_STEP, HAS2_TWO, HAS3_ZERO, HAS3_STEP = range(16, 23)
FIX_LEFT, FIX_RIGHT, OTHER, RELAY_OWN = 23, 24, 25, 26
META = 27


def wrap(value, size):
    value = jnp.where(value >= size, value - size, value)
    return jnp.where(value < 0, value + size, value)


def structure_kernel(place_ref, xcol_ref, mcol_ref, count_ref, out_ref):
    row, col = place_ref[0], place_ref[1]
    second, third = lax.rem(row, GY), lax.div(row, GY)

    def column(a, b, c):
        return wrap(a, GX) + GX * (wrap(b, GY) + GY * wrap(c, GZ))

    def holds(place, target):
        found = jnp.int32(0)
        count = count_ref[place]
        for m in range(SLOTS):
            hit = jnp.logical_and(count > m, mcol_ref[m, place] == target)
            found = found + hit.astype(jnp.int32)
        return found

    for r in range(2):
        first = 2 * col + r
        me = column(first, second, third)
        pos1 = xcol_ref[1, me] == column(first + 1, second, third)
        pos2 = xcol_ref[2, me] == column(first, second + 1, third)
        pos3 = xcol_ref[3, me] == column(first, second, third + 1)
        s1, s2, s3 = (jnp.where(p, 1, -1) for p in (pos1, pos2, pos3))
        f1, f2, f3 = wrap(first + s1, GX), wrap(second + s2, GY), wrap(third + s3, GZ)
        c1, c2, c3 = column(f1, second, third), column(first, f2, third), column(first, second, f3)
        far2 = column(first, f2 + s2, third)
        npos1 = xcol_ref[1, c1] == column(f1 + 1, second, third)
        npos2 = xcol_ref[2, c2] == column(first, f2 + 1, third)
        npos3 = xcol_ref[3, c3] == column(first, second, f3 + 1)
        fpos2 = xcol_ref[2, far2] == column(first, f2 + s2 + 1 - jnp.where(f2 + s2 >= GY, GY, 0), third)
        even = lax.rem(second, 2) == 0
        for place, flag in (
            (POS1, pos1),
            (POS2, pos2),
            (POS3, pos3),
            (NPOS1, npos1),
            (NPOS2, npos2),
            (NPOS3, npos3),
            (FPOS2, fpos2),
            (NEAR2, pos2 == even),
        ):
            out_ref[r, place] = flag.astype(jnp.int32)
        count = count_ref[me]
        for k, (a, b, c) in enumerate(OFFSETS):
            target = column(first + a, second + b, third + c)
            slot = jnp.int32(-1)
            for m in range(SLOTS):
                hit = jnp.logical_and(count > m, mcol_ref[m, me] == target)
                slot = jnp.where(hit, m, slot)
            out_ref[r, SLOT_OF + k] = slot
        n1, n2 = jnp.where(npos1, 1, -1), jnp.where(npos2, 1, -1)
        out_ref[r, HAS1_ZERO] = holds(c1, c1)
        out_ref[r, HAS1_STEP] = holds(c1, column(f1 + n1, second, third))
        out_ref[r, HAS2_ZERO] = holds(c2, c2)
        out_ref[r, HAS2_STEP] = holds(c2, column(first, f2 + n2, third))
        out_ref[r, HAS2_TWO] = holds(c2, column(first, f2 + 2, third))
        out_ref[r, HAS3_ZERO] = holds(c3, c3)
        out_ref[r, HAS3_STEP] = holds(c3, column(first, second, f3 + 1))
        out_ref[r, OTHER] = 1 - lax.rem(row, 2)
        odd = lax.rem(third, 2)
        partner = third + 1 - 2 * odd
        wants_up = xcol_ref[3, column(first, second, partner)] == column(first, second, partner + 1)
        out_ref[r, RELAY_OWN] = (wants_up == (odd == 1)).astype(jnp.int32)
        out_ref[r, FIX_LEFT] = (lax.rem(col, RING) == 0).astype(jnp.int32)
        out_ref[r, FIX_RIGHT] = (lax.rem(col, RING) == RING - 1).astype(jnp.int32)


def halves(value):
    high = value.astype(jnp.bfloat16)
    low = (value - high.astype(jnp.float32)).astype(jnp.bfloat16)
    return high, low


def left(value):
    high, low = halves(value)
    return jnp.concatenate([high, low, high], axis=1)


def right(value):
    high, low = halves(value)
    return jnp.concatenate([high, high, low], axis=0)


def product(lefts, rights):
    a = lefts[0] if len(lefts) == 1 else jnp.concatenate(lefts, axis=1)
    b = rights[0] if len(rights) == 1 else jnp.concatenate(rights, axis=0)
    return jnp.dot(a, b, preferred_element_type=jnp.float32)


def row_view(meta, r):
    flag = lambda k: meta[r, k] != 0
    slot = lambda k: meta[r, SLOT_OF + k]
    return flag, slot


def from_side(flag, fix, ring, wraps, k):
    wrap, place = ((0, 0), (0, 1), (1, 0), (0, 2))[k]
    return jnp.where(flag(fix), wraps[wrap][place], ring[k])


def first_neighbour(r, flag, x, ring_left, ring_right, wraps):
    blocks = []
    for k in range(2):
        up = x[1, k] if r == 0 else from_side(flag, FIX_RIGHT, ring_right, wraps, k)
        down = from_side(flag, FIX_LEFT, ring_left, wraps, k) if r == 0 else x[0, k]
        blocks.append(jnp.where(flag(POS1), up, down))
    return blocks


def second_neighbour(meta, r, flag, near, across):
    other = meta[0, OTHER]
    return [jnp.where(flag(NEAR2), near[other, k, r], across[other, k, r]) for k in range(2)]


def edge_kernel(place, x, arrived, edge):
    del arrived
    last = lax.rem(place[1], RING) == RING - 1
    for k in range(2):
        edge[k] = jnp.where(last, x[1, k], x[0, k])
    edge[2] = x[1, 0]


def base_kernel(
    meta, x, near, across, above, below, relayed, base, third, to_left, to_right, to_wrap, handed
):
    to_left[0:2] = x[0, 0:2]
    to_left[3] = x[1, 0]
    to_right[0:2] = x[1, 0:2]
    inside = jnp.logical_and(meta[0, POS1] != 0, meta[1, POS1] == 0)
    for r in range(2):
        flag, _ = row_view(meta, r)
        d, a1, a2, a3 = (x[r, s] for s in range(4))
        _, b2 = second_neighbour(meta, r, flag, near, across)
        b3 = jnp.where(flag(POS3), above[r], below[r])
        handed[r] = jnp.where(flag(RELAY_OWN), d, relayed[r])
        third[r] = b3
        rights = [right(x[1 - r, 1]), right(b2), right(b3)]
        mutual = [inside] + [flag(POS1 + k) != flag(NPOS1 + k) for k in (1, 2)]
        none = jnp.zeros_like(rights[0])
        value = product(
            [left(d), left(a1), left(a2), left(a3)],
            [right(d)] + [jnp.where(m, b, none) for m, b in zip(mutual, rights)],
        )
        base[r] = value
        (to_left if r == 0 else to_right)[2] = value
        if r == 0:
            to_wrap[0] = value
        else:

            @pl.when(flag(FIX_RIGHT))
            def _():
                to_wrap[0] = value


def early_kernel(
    meta, x, near, across, opposite, to_wrap, handed, square, cube, wrap_message, third_message
):
    wrap_message[...] = to_wrap[...]
    third_message[...] = handed[...]
    square[...] = jnp.zeros_like(square)
    cube[...] = jnp.zeros_like(cube)
    for r in range(2):
        flag, slot = row_view(meta, r)
        pos2, npos2 = flag(POS2), flag(NPOS2)
        d, a2 = x[r, 0], x[r, 2]
        d2, b2 = second_neighbour(meta, r, flag, near, across)
        ld, l2, r2 = left(d), left(a2), right(b2)

        def put(where, value):
            square[r, where] = value
            cube[r, where] += product([ld], [right(value)])

        step2 = jnp.where(pos2, slot(UP2), slot(DOWN2))
        back2 = jnp.where(pos2, slot(DOWN2), slot(UP2))
        mutual2 = pos2 != npos2
        other2 = jnp.where(mutual2, slot(ZERO), slot(TWO2))

        @pl.when(step2 >= 0)
        def _():
            put(step2, product([ld, l2], [right(a2), right(d2)]))

        @pl.when(jnp.logical_and(slot(TWO2) >= 0, jnp.logical_not(mutual2)))
        def _():
            put(slot(TWO2), product([l2], [r2]))

        @pl.when(jnp.logical_and(other2 >= 0, flag(HAS2_STEP)))
        def _():
            beyond = jnp.where(mutual2, d, opposite[0, r])
            step = product([left(d2), left(b2)], [r2, right(beyond)])
            cube[r, other2] += product([l2], [right(step)])

        onward2 = jnp.logical_and(jnp.logical_not(mutual2), npos2 == flag(FPOS2))

        @pl.when(jnp.logical_and(onward2, jnp.logical_and(back2 >= 0, flag(HAS2_TWO))))
        def _():
            two = product([left(b2)], [right(opposite[1, r])])
            cube[r, back2] += product([l2], [right(two)])


def copy_kernel(given, taken):
    taken[...] = given[...]


def meeting(flag, r):
    away = flag(POS1) if r == 1 else jnp.logical_not(flag(POS1))
    return away, jnp.logical_and(away, flag(POS1) != flag(NPOS1))


def side_block(flag, r, ring_left, ring_right, wraps, k):
    fix, ring = (FIX_LEFT, ring_left) if r == 0 else (FIX_RIGHT, ring_right)
    return from_side(flag, fix, ring, wraps, k)


def middle_kernel(meta, x, base, ring_left, ring_right, wrap_a, middle):
    for r in range(2):
        flag, _ = row_view(meta, r)
        _, met = meeting(flag, r)
        b1 = side_block(flag, r, ring_left, ring_right, (wrap_a,), 1)
        added = product([left(x[r, 1])], [right(b1)])
        middle[r] = base[r] + jnp.where(met, added, jnp.zeros_like(added))


def late_kernel(
    meta,
    x,
    early,
    early_part,
    middle,
    ring_left,
    ring_right,
    wrap_a,
    wrap_b,
    third,
    third_d,
    square,
    cube,
):
    wraps = (wrap_a, wrap_b)
    square[...] = early[...]
    cube[...] = early_part[...]
    for r in range(2):
        flag, slot = row_view(meta, r)
        pos1, pos3, npos1 = flag(POS1), flag(POS3), flag(NPOS1)
        d, a1 = x[r, 0], x[r, 1]
        d1, b1 = first_neighbour(r, flag, x, ring_left, ring_right, wraps)
        ld, l1, r1 = left(d), left(a1), right(b1)

        def put(where, value):
            square[r, where] = value
            cube[r, where] += product([ld], [right(value)])

        step1 = jnp.where(pos1, slot(UP1), slot(DOWN1))

        @pl.when(slot(ZERO) >= 0)
        def _():
            put(slot(ZERO), middle[r])

        @pl.when(step1 >= 0)
        def _():
            put(step1, product([ld, l1], [right(a1), right(d1)]))

        @pl.when(jnp.logical_and(slot(TWO1) >= 0, jnp.logical_and(pos1, npos1)))
        def _():
            put(slot(TWO1), product([l1], [r1]))

        mutual1 = pos1 != npos1
        other1 = jnp.where(mutual1, slot(ZERO), jnp.where(pos1, slot(TWO1), -1))

        @pl.when(jnp.logical_and(step1 >= 0, flag(HAS1_ZERO)))
        def _():
            away, met = meeting(flag, r)
            back = product([left(b1)], [right(a1)])
            outer = side_block(flag, r, ring_left, ring_right, wraps, 2)
            outer += jnp.where(met, back, jnp.zeros_like(back))
            cube[r, step1] += product([l1], [right(jnp.where(away, outer, middle[1 - r]))])

        @pl.when(jnp.logical_and(other1 >= 0, flag(HAS1_STEP)))
        def _():
            far = from_side(flag, FIX_RIGHT, ring_right, wraps, 3 * r)
            beyond = jnp.where(mutual1, d, far)
            step = product([left(d1), left(b1)], [r1, right(beyond)])
            cube[r, other1] += product([l1], [right(step)])

        back3 = jnp.logical_and(jnp.logical_not(pos3), flag(NPOS3))

        @pl.when(jnp.logical_and(back3, jnp.logical_and(slot(ZERO) >= 0, flag(HAS3_STEP))))
        def _():
            b3 = third[r]
            step = product([left(third_d[r]), left(b3)], [right(b3), right(d)])
            cube[r, slot(ZERO)] += product([left(x[r, 3])], [right(step)])

        @pl.when(jnp.logical_and(slot(UP3) >= 0, pos3))
        def _():
            a3 = x[r, 3]
            put(slot(UP3), product([ld, left(a3)], [right(a3), right(third_d[r])]))


def cube_kernel(meta, x, part, mid_near, mid_across, mid_above, cube):
    cube[...] = part[...]
    for r in range(2):
        flag, slot = row_view(meta, r)
        step2 = jnp.where(flag(POS2), slot(UP2), slot(DOWN2))

        @pl.when(jnp.logical_and(step2 >= 0, flag(HAS2_ZERO)))
        def _():
            value = jnp.where(flag(NEAR2), mid_near[meta[0, OTHER], r], mid_across[r])
            cube[r, step2] += product([left(x[r, 2])], [right(value)])

        ahead = jnp.logical_and(flag(POS3), flag(HAS3_ZERO))

        @pl.when(jnp.logical_and(ahead, slot(UP3) >= 0))
        def _():
            cube[r, slot(UP3)] += product([left(x[r, 3])], [right(mid_above[r])])


def call(kernel, out_shapes, *operands, smem=0, free=0, smem_out=False, flops=0):
    held = len(operands) - smem - free
    spaces = [pltpu.SMEM] * smem + [pltpu.VMEM] * held + [pl.ANY] * free
    out_space = pltpu.SMEM if smem_out else pltpu.VMEM
    return pl.pallas_call(
        kernel,
        out_shape=out_shapes,
        in_specs=[pl.BlockSpec(memory_space=s) for s in spaces],
        out_specs=jax.tree.map(lambda _: pl.BlockSpec(memory_space=out_space), out_shapes),
        compiler_params=pltpu.CompilerParams(vmem_limit_bytes=32 * 2**20),
        cost_estimate=pl.CostEstimate(flops=flops, bytes_accessed=2**21, transcendentals=0),
    )(*operands)


def per_device(x, x_cols, mask_cols, mask_count):
    row_count, col_count = lax.axis_size("row"), lax.axis_size("col")
    row, col = lax.axis_index("row"), lax.axis_index("col")

    def along(value, axis, target, count):
        return lax.ppermute(value, axis, [(i, target(i) % count) for i in range(count)])

    def anywhere(value, target):
        pairs = []
        for i in range(row_count * col_count):
            there = target(i // col_count, i % col_count)
            if there is not None:
                pairs.append((i, there[0] * col_count + there[1] % col_count))
        return lax.ppermute(value, ("row", "col"), pairs)

    def to_col(value, step):
        def target(i, j):
            return (i, j + step) if j // RING == (j + step) // RING else None

        return anywhere(value, target)

    def to_wrap(value):
        return anywhere(value, lambda i, j: {0: (i, j - 1), RING - 1: (i, j + 1)}.get(j % RING))

    def to_row(value, step):
        return along(value, "row", lambda i: i + step, row_count)

    def flip_row(value, bits):
        return along(value, "row", lambda i: i ^ bits, row_count)

    def both_cores(value):
        groups = [[i, i + 1] for i in range(0, row_count, 2)]
        return lax.all_gather(value, "row", axis_index_groups=groups)

    block = lambda *lead: jax.ShapeDtypeStruct(lead + (BS, BS), jnp.float32)

    place = jnp.stack([row, col]).astype(jnp.int32)
    pair2 = jnp.stack([x[:, 0], x[:, 2]])
    opposite = flip_row(pair2, 2)
    above = to_row(x[:, 3], -GY)
    below = to_row(x[:, 3], GY)
    edge = call(edge_kernel, block(3), place, x, opposite, smem=1, free=1)
    wrap_a = call(copy_kernel, block(3), to_wrap(edge), flops=FIRST_FLOPS)
    relayed = along(x[:, 0], "row", lambda i: i + 2 * GY * (2 * (i // GY % 2) - 1), row_count)
    near = both_cores(pair2)
    across = both_cores(opposite)

    meta = call(
        structure_kernel,
        jax.ShapeDtypeStruct((2, META), jnp.int32),
        *(place, x_cols.T, mask_cols.T, mask_count),
        smem=4,
        smem_out=True,
    )
    base, third, left_message, right_message, wrap_message, handed = call(
        base_kernel,
        [block(2), block(2), block(4), block(3), block(1), block(2)],
        *(meta, x, near, across, above, below, relayed),
        smem=1,
        flops=24 * 2 * BS**3,
    )
    ring_right = to_col(left_message, -1)
    ring_left = to_col(right_message, 1)
    early, early_part, wrap_message, handed = call(
        early_kernel,
        [block(2, SLOTS), block(2, SLOTS), block(1), block(2)],
        *(meta, x, near, across, opposite, wrap_message, handed),
        smem=1,
        flops=60 * 2 * BS**3,
    )
    wrap_b = to_wrap(wrap_message)
    third_d = flip_row(handed, GY)
    middle = call(
        middle_kernel,
        block(2),
        *(meta, x, base, ring_left, ring_right, wrap_a),
        smem=1,
        flops=6 * 2 * BS**3,
    )
    mid_above = to_row(middle, -GY)
    mid_across = flip_row(middle, 3)
    mid_near = both_cores(middle)
    square, part = call(
        late_kernel,
        [block(2, SLOTS), block(2, SLOTS)],
        *(meta, x, early, early_part, middle, ring_left, ring_right),
        *(wrap_a, wrap_b, third, third_d),
        smem=1,
        flops=60 * 2 * BS**3,
    )
    cube = call(
        cube_kernel,
        block(2, SLOTS),
        *(meta, x, part, mid_near, mid_across, mid_above),
        smem=1,
        flops=12 * 2 * BS**3,
    )
    return square, cube


def solution(mesh):
    in_specs = (P(("row", "col"), None, None, None), P(), P(), P())
    out_specs = (P(("row", "col"), None, None, None), P(("row", "col"), None, None, None))
    return jax.shard_map(
        per_device, mesh=mesh, in_specs=in_specs, out_specs=out_specs, check_vma=False
    )
```

```python
import jax
import jax.numpy as jnp
from jax import lax
from jax.experimental import pallas as pl
from jax.experimental.pallas import tpu as pltpu
from jax.sharding import PartitionSpec as P

GX, GY, GZ = 48, 4, 8
BS = 128
SLOTS = 6
FIRST_FLOPS = 24 * 10**8
RING = 8

ZERO, UP1, DOWN1, TWO1, UP2, DOWN2, TWO2, UP3 = range(8)
OFFSETS = ((0, 0, 0), (1, 0, 0), (-1, 0, 0), (2, 0, 0), (0, 1, 0), (0, -1, 0), (0, 2, 0), (0, 0, 1))

POS1, POS2, POS3, NPOS1, NPOS2, NPOS3, FPOS2, NEAR2 = range(8)
SLOT_OF = 8
HAS1_ZERO, HAS1_STEP, HAS2_ZERO, HAS2_STEP, HAS2_TWO, HAS3_ZERO, HAS3_STEP = range(16, 23)
FIX_LEFT, FIX_RIGHT, OTHER, RELAY_OWN = 23, 24, 25, 26
META = 27


def wrap(value, size):
    value = jnp.where(value >= size, value - size, value)
    return jnp.where(value < 0, value + size, value)


def structure_kernel(place_ref, xcol_ref, mcol_ref, count_ref, out_ref):
    row, col = place_ref[0], place_ref[1]
    second, third = lax.rem(row, GY), lax.div(row, GY)

    def column(a, b, c):
        return wrap(a, GX) + GX * (wrap(b, GY) + GY * wrap(c, GZ))

    def holds(place, target):
        found = jnp.int32(0)
        count = count_ref[place]
        for m in range(SLOTS):
            hit = jnp.logical_and(count > m, mcol_ref[m, place] == target)
            found = found + hit.astype(jnp.int32)
        return found

    for r in range(2):
        first = 2 * col + r
        me = column(first, second, third)
        pos1 = xcol_ref[1, me] == column(first + 1, second, third)
        pos2 = xcol_ref[2, me] == column(first, second + 1, third)
        pos3 = xcol_ref[3, me] == column(first, second, third + 1)
        s1, s2, s3 = (jnp.where(p, 1, -1) for p in (pos1, pos2, pos3))
        f1, f2, f3 = wrap(first + s1, GX), wrap(second + s2, GY), wrap(third + s3, GZ)
        c1, c2, c3 = column(f1, second, third), column(first, f2, third), column(first, second, f3)
        far2 = column(first, f2 + s2, third)
        npos1 = xcol_ref[1, c1] == column(f1 + 1, second, third)
        npos2 = xcol_ref[2, c2] == column(first, f2 + 1, third)
        npos3 = xcol_ref[3, c3] == column(first, second, f3 + 1)
        fpos2 = xcol_ref[2, far2] == column(first, f2 + s2 + 1 - jnp.where(f2 + s2 >= GY, GY, 0), third)
        even = lax.rem(second, 2) == 0
        for place, flag in (
            (POS1, pos1),
            (POS2, pos2),
            (POS3, pos3),
            (NPOS1, npos1),
            (NPOS2, npos2),
            (NPOS3, npos3),
            (FPOS2, fpos2),
            (NEAR2, pos2 == even),
        ):
            out_ref[r, place] = flag.astype(jnp.int32)
        count = count_ref[me]
        for k, (a, b, c) in enumerate(OFFSETS):
            target = column(first + a, second + b, third + c)
            slot = jnp.int32(-1)
            for m in range(SLOTS):
                hit = jnp.logical_and(count > m, mcol_ref[m, me] == target)
                slot = jnp.where(hit, m, slot)
            out_ref[r, SLOT_OF + k] = slot
        n1, n2 = jnp.where(npos1, 1, -1), jnp.where(npos2, 1, -1)
        out_ref[r, HAS1_ZERO] = holds(c1, c1)
        out_ref[r, HAS1_STEP] = holds(c1, column(f1 + n1, second, third))
        out_ref[r, HAS2_ZERO] = holds(c2, c2)
        out_ref[r, HAS2_STEP] = holds(c2, column(first, f2 + n2, third))
        out_ref[r, HAS2_TWO] = holds(c2, column(first, f2 + 2, third))
        out_ref[r, HAS3_ZERO] = holds(c3, c3)
        out_ref[r, HAS3_STEP] = holds(c3, column(first, second, f3 + 1))
        out_ref[r, OTHER] = 1 - lax.rem(row, 2)
        odd = lax.rem(third, 2)
        partner = third + 1 - 2 * odd
        wants_up = xcol_ref[3, column(first, second, partner)] == column(first, second, partner + 1)
        out_ref[r, RELAY_OWN] = (wants_up == (odd == 1)).astype(jnp.int32)
        out_ref[r, FIX_LEFT] = (lax.rem(col, RING) == 0).astype(jnp.int32)
        out_ref[r, FIX_RIGHT] = (lax.rem(col, RING) == RING - 1).astype(jnp.int32)


def halves(value):
    high = value.astype(jnp.bfloat16)
    low = (value - high.astype(jnp.float32)).astype(jnp.bfloat16)
    return high, low


def left(value):
    return jnp.concatenate(halves(value), axis=0)


def right(value):
    return jnp.concatenate(halves(value), axis=1)


def product(lefts, rights):
    a = lefts[0] if len(lefts) == 1 else jnp.concatenate(lefts, axis=1)
    b = rights[0] if len(rights) == 1 else jnp.concatenate(rights, axis=0)
    all_four = jnp.dot(a, b, preferred_element_type=jnp.float32)
    small = all_four[:BS, BS:] + all_four[BS:, :BS]
    return all_four[:BS, :BS] + (small + all_four[BS:, BS:])


def row_view(meta, r):
    flag = lambda k: meta[r, k] != 0
    slot = lambda k: meta[r, SLOT_OF + k]
    return flag, slot


def from_side(flag, fix, ring, wraps, k):
    wrap, place = ((0, 0), (0, 1), (1, 0), (0, 2))[k]
    return jnp.where(flag(fix), wraps[wrap][place], ring[k])


def first_neighbour(r, flag, x, ring_left, ring_right, wraps):
    blocks = []
    for k in range(2):
        up = x[1, k] if r == 0 else from_side(flag, FIX_RIGHT, ring_right, wraps, k)
        down = from_side(flag, FIX_LEFT, ring_left, wraps, k) if r == 0 else x[0, k]
        blocks.append(jnp.where(flag(POS1), up, down))
    return blocks


def second_neighbour(meta, r, flag, near, across):
    other = meta[0, OTHER]
    return [jnp.where(flag(NEAR2), near[other, k, r], across[other, k, r]) for k in range(2)]


def edge_kernel(place, x, arrived, edge):
    del arrived
    last = lax.rem(place[1], RING) == RING - 1
    for k in range(2):
        edge[k] = jnp.where(last, x[1, k], x[0, k])
    edge[2] = x[1, 0]


def base_kernel(
    meta, x, near, across, above, below, relayed, base, third, to_left, to_right, to_wrap, handed
):
    to_left[0:2] = x[0, 0:2]
    to_left[3] = x[1, 0]
    to_right[0:2] = x[1, 0:2]
    inside = jnp.logical_and(meta[0, POS1] != 0, meta[1, POS1] == 0)
    for r in range(2):
        flag, _ = row_view(meta, r)
        d, a1, a2, a3 = (x[r, s] for s in range(4))
        _, b2 = second_neighbour(meta, r, flag, near, across)
        b3 = jnp.where(flag(POS3), above[r], below[r])
        handed[r] = jnp.where(flag(RELAY_OWN), d, relayed[r])
        third[r] = b3
        rights = [right(x[1 - r, 1]), right(b2), right(b3)]
        mutual = [inside] + [flag(POS1 + k) != flag(NPOS1 + k) for k in (1, 2)]
        none = jnp.zeros_like(rights[0])
        value = product(
            [left(d), left(a1), left(a2), left(a3)],
            [right(d)] + [jnp.where(m, b, none) for m, b in zip(mutual, rights)],
        )
        base[r] = value
        (to_left if r == 0 else to_right)[2] = value
        if r == 0:
            to_wrap[0] = value
        else:

            @pl.when(flag(FIX_RIGHT))
            def _():
                to_wrap[0] = value


def early_kernel(
    meta, x, near, across, opposite, to_wrap, handed, square, cube, wrap_message, third_message
):
    wrap_message[...] = to_wrap[...]
    third_message[...] = handed[...]
    square[...] = jnp.zeros_like(square)
    cube[...] = jnp.zeros_like(cube)
    results = []
    for r in range(2):
        flag, _ = row_view(meta, r)
        mutual2 = flag(POS2) != flag(NPOS2)
        d, a2 = x[r, 0], x[r, 2]
        d2, b2 = second_neighbour(meta, r, flag, near, across)
        ld, l2, lb, r2 = left(d), left(a2), left(b2), right(b2)
        once = product([ld, l2], [right(a2), right(d2)])
        twice = product([l2], [r2])
        beyond = jnp.where(mutual2, d, opposite[0, r])
        step = right(product([left(d2), lb], [r2, right(beyond)]))
        two = product([lb], [right(opposite[1, r])])
        ahead = jnp.where(flag(HAS2_STEP), step, jnp.zeros_like(step))
        results.append(
            (
                once,
                twice,
                product([ld], [right(once)]),
                product([ld, l2], [right(twice), ahead]),
                product([l2], [step]),
                product([l2], [right(two)]),
            )
        )
    for r, (once, twice, cube_once, cube_twice, cube_zero, cube_back) in enumerate(results):
        flag, slot = row_view(meta, r)
        pos2, npos2 = flag(POS2), flag(NPOS2)
        mutual2 = pos2 != npos2
        step2 = jnp.where(pos2, slot(UP2), slot(DOWN2))
        back2 = jnp.where(pos2, slot(DOWN2), slot(UP2))

        @pl.when(step2 >= 0)
        def _():
            square[r, step2] = once
            cube[r, step2] = cube_once

        @pl.when(jnp.logical_and(slot(TWO2) >= 0, jnp.logical_not(mutual2)))
        def _():
            square[r, slot(TWO2)] = twice
            cube[r, slot(TWO2)] = cube_twice

        @pl.when(jnp.logical_and(slot(ZERO) >= 0, jnp.logical_and(mutual2, flag(HAS2_STEP))))
        def _():
            cube[r, slot(ZERO)] = cube_zero

        onward2 = jnp.logical_and(jnp.logical_not(mutual2), npos2 == flag(FPOS2))

        @pl.when(jnp.logical_and(onward2, jnp.logical_and(back2 >= 0, flag(HAS2_TWO))))
        def _():
            cube[r, back2] = cube_back


def copy_kernel(given, taken):
    taken[...] = given[...]


def meeting(flag, r):
    away = flag(POS1) if r == 1 else jnp.logical_not(flag(POS1))
    return away, jnp.logical_and(away, flag(POS1) != flag(NPOS1))


def side_block(flag, r, ring_left, ring_right, wraps, k):
    fix, ring = (FIX_LEFT, ring_left) if r == 0 else (FIX_RIGHT, ring_right)
    return from_side(flag, fix, ring, wraps, k)


def middle_kernel(meta, x, base, ring_left, ring_right, wrap_a, middle):
    for r in range(2):
        flag, _ = row_view(meta, r)
        _, met = meeting(flag, r)
        b1 = side_block(flag, r, ring_left, ring_right, (wrap_a,), 1)
        added = product([left(x[r, 1])], [right(b1)])
        middle[r] = base[r] + jnp.where(met, added, jnp.zeros_like(added))


def late_kernel(
    meta,
    x,
    early,
    early_part,
    middle,
    ring_left,
    ring_right,
    wrap_a,
    wrap_b,
    third,
    third_d,
    square,
    cube,
):
    wraps = (wrap_a, wrap_b)
    square[...] = early[...]
    cube[...] = early_part[...]
    results = []
    for r in range(2):
        flag, _ = row_view(meta, r)
        pos1, pos3 = flag(POS1), flag(POS3)
        mutual1 = pos1 != flag(NPOS1)
        d, a1, a3 = x[r, 0], x[r, 1], x[r, 3]
        d1, b1 = first_neighbour(r, flag, x, ring_left, ring_right, wraps)
        d3, b3 = third_d[r], third[r]
        ld, l1, l3, lb, r1 = left(d), left(a1), left(a3), left(b1), right(b1)
        ra1, rd = right(a1), right(d)
        once = product([ld, l1], [ra1, right(d1)])
        twice = product([l1], [r1])
        up = product([ld, l3], [right(a3), right(d3)])
        far = from_side(flag, FIX_RIGHT, ring_right, wraps, 3 * r)
        step = right(product([left(d1), lb], [r1, right(jnp.where(mutual1, d, far))]))
        step3 = right(product([left(d3), left(b3)], [right(b3), rd]))
        away, met = meeting(flag, r)
        back = product([lb], [ra1])
        outer = side_block(flag, r, ring_left, ring_right, wraps, 2)
        outer += jnp.where(met, back, jnp.zeros_like(back))
        beside = right(jnp.where(away, outer, middle[1 - r]))
        none = jnp.zeros_like(step)
        beside = jnp.where(flag(HAS1_ZERO), beside, none)
        step = jnp.where(flag(HAS1_STEP), step, none)
        back3 = jnp.logical_and(jnp.logical_not(pos3), flag(NPOS3))
        step3 = jnp.where(jnp.logical_and(back3, flag(HAS3_STEP)), step3, none)
        zero = [right(middle[r]), jnp.where(mutual1, step, none), step3]
        results.append(
            (
                once,
                twice,
                up,
                product([ld, l1], [right(once), beside]),
                product([ld, l1], [right(twice), step]),
                product([ld], [right(up)]),
                product([ld, l1, l3], zero),
            )
        )
    for r, (once, twice, up, cube_once, cube_twice, cube_up, cube_zero) in enumerate(results):
        flag, slot = row_view(meta, r)
        pos1 = flag(POS1)
        step1 = jnp.where(pos1, slot(UP1), slot(DOWN1))

        @pl.when(slot(ZERO) >= 0)
        def _():
            square[r, slot(ZERO)] = middle[r]
            cube[r, slot(ZERO)] += cube_zero

        @pl.when(step1 >= 0)
        def _():
            square[r, step1] = once
            cube[r, step1] = cube_once

        @pl.when(jnp.logical_and(slot(TWO1) >= 0, jnp.logical_and(pos1, flag(NPOS1))))
        def _():
            square[r, slot(TWO1)] = twice
            cube[r, slot(TWO1)] = cube_twice

        @pl.when(jnp.logical_and(slot(UP3) >= 0, flag(POS3)))
        def _():
            square[r, slot(UP3)] = up
            cube[r, slot(UP3)] = cube_up


def cube_kernel(meta, x, part, mid_near, mid_across, mid_above, cube):
    cube[...] = part[...]
    added = []
    for r in range(2):
        flag, _ = row_view(meta, r)
        value = jnp.where(flag(NEAR2), mid_near[meta[0, OTHER], r], mid_across[r])
        added.append(
            (
                product([left(x[r, 2])], [right(value)]),
                product([left(x[r, 3])], [right(mid_above[r])]),
            )
        )
    for r, (beside, above) in enumerate(added):
        flag, slot = row_view(meta, r)
        step2 = jnp.where(flag(POS2), slot(UP2), slot(DOWN2))

        @pl.when(jnp.logical_and(step2 >= 0, flag(HAS2_ZERO)))
        def _():
            cube[r, step2] += beside

        ahead = jnp.logical_and(flag(POS3), flag(HAS3_ZERO))

        @pl.when(jnp.logical_and(ahead, slot(UP3) >= 0))
        def _():
            cube[r, slot(UP3)] += above


def call(kernel, out_shapes, *operands, smem=0, free=0, smem_out=False, flops=0):
    held = len(operands) - smem - free
    spaces = [pltpu.SMEM] * smem + [pltpu.VMEM] * held + [pl.ANY] * free
    out_space = pltpu.SMEM if smem_out else pltpu.VMEM
    return pl.pallas_call(
        kernel,
        out_shape=out_shapes,
        in_specs=[pl.BlockSpec(memory_space=s) for s in spaces],
        out_specs=jax.tree.map(lambda _: pl.BlockSpec(memory_space=out_space), out_shapes),
        compiler_params=pltpu.CompilerParams(vmem_limit_bytes=32 * 2**20),
        cost_estimate=pl.CostEstimate(flops=flops, bytes_accessed=2**21, transcendentals=0),
    )(*operands)


def per_device(x, x_cols, mask_cols, mask_count):
    row_count, col_count = lax.axis_size("row"), lax.axis_size("col")
    row, col = lax.axis_index("row"), lax.axis_index("col")

    def along(value, axis, target, count):
        return lax.ppermute(value, axis, [(i, target(i) % count) for i in range(count)])

    def anywhere(value, target):
        pairs = []
        for i in range(row_count * col_count):
            there = target(i // col_count, i % col_count)
            if there is not None:
                pairs.append((i, there[0] * col_count + there[1] % col_count))
        return lax.ppermute(value, ("row", "col"), pairs)

    def to_col(value, step):
        def target(i, j):
            return (i, j + step) if j // RING == (j + step) // RING else None

        return anywhere(value, target)

    def to_wrap(value):
        return anywhere(value, lambda i, j: {0: (i, j - 1), RING - 1: (i, j + 1)}.get(j % RING))

    def to_row(value, step):
        return along(value, "row", lambda i: i + step, row_count)

    def flip_row(value, bits):
        return along(value, "row", lambda i: i ^ bits, row_count)

    def both_cores(value):
        groups = [[i, i + 1] for i in range(0, row_count, 2)]
        return lax.all_gather(value, "row", axis_index_groups=groups)

    block = lambda *lead: jax.ShapeDtypeStruct(lead + (BS, BS), jnp.float32)

    place = jnp.stack([row, col]).astype(jnp.int32)
    pair2 = jnp.stack([x[:, 0], x[:, 2]])
    opposite = flip_row(pair2, 2)
    above = to_row(x[:, 3], -GY)
    below = to_row(x[:, 3], GY)
    edge = call(edge_kernel, block(3), place, x, opposite, smem=1, free=1)
    wrap_a = call(copy_kernel, block(3), to_wrap(edge), flops=FIRST_FLOPS)
    relayed = along(x[:, 0], "row", lambda i: i + 2 * GY * (2 * (i // GY % 2) - 1), row_count)
    near = both_cores(pair2)
    across = both_cores(opposite)

    meta = call(
        structure_kernel,
        jax.ShapeDtypeStruct((2, META), jnp.int32),
        *(place, x_cols.T, mask_cols.T, mask_count),
        smem=4,
        smem_out=True,
    )
    base, third, left_message, right_message, wrap_message, handed = call(
        base_kernel,
        [block(2), block(2), block(4), block(3), block(1), block(2)],
        *(meta, x, near, across, above, below, relayed),
        smem=1,
        flops=24 * 2 * BS**3,
    )
    ring_right = to_col(left_message, -1)
    ring_left = to_col(right_message, 1)
    early, early_part, wrap_message, handed = call(
        early_kernel,
        [block(2, SLOTS), block(2, SLOTS), block(1), block(2)],
        *(meta, x, near, across, opposite, wrap_message, handed),
        smem=1,
        flops=60 * 2 * BS**3,
    )
    wrap_b = to_wrap(wrap_message)
    third_d = flip_row(handed, GY)
    middle = call(
        middle_kernel,
        block(2),
        *(meta, x, base, ring_left, ring_right, wrap_a),
        smem=1,
        flops=6 * 2 * BS**3,
    )
    mid_above = to_row(middle, -GY)
    mid_across = flip_row(middle, 3)
    mid_near = both_cores(middle)
    square, part = call(
        late_kernel,
        [block(2, SLOTS), block(2, SLOTS)],
        *(meta, x, early, early_part, middle, ring_left, ring_right),
        *(wrap_a, wrap_b, third, third_d),
        smem=1,
        flops=60 * 2 * BS**3,
    )
    cube = call(
        cube_kernel,
        block(2, SLOTS),
        *(meta, x, part, mid_near, mid_across, mid_above),
        smem=1,
        flops=12 * 2 * BS**3,
    )
    return square, cube


def solution(mesh):
    in_specs = (P(("row", "col"), None, None, None), P(), P(), P())
    out_specs = (P(("row", "col"), None, None, None), P(("row", "col"), None, None, None))
    return jax.shard_map(
        per_device, mesh=mesh, in_specs=in_specs, out_specs=out_specs, check_vma=False
    )
```

```python
import jax
import jax.numpy as jnp
from jax import lax
from jax.experimental import pallas as pl
from jax.experimental.pallas import tpu as pltpu
from jax.sharding import PartitionSpec as P

GX, GY, GZ = 48, 4, 8
BS = 128
SLOTS = 6
FIRST_FLOPS = 24 * 10**8
RING = 8

ZERO, UP1, DOWN1, TWO1, UP2, DOWN2, TWO2, UP3 = range(8)
OFFSETS = ((0, 0, 0), (1, 0, 0), (-1, 0, 0), (2, 0, 0), (0, 1, 0), (0, -1, 0), (0, 2, 0), (0, 0, 1))

POS1, POS2, POS3, NPOS1, NPOS2, NPOS3, FPOS2, NEAR2 = range(8)
SLOT_OF = 8
HAS1_ZERO, HAS1_STEP, HAS2_ZERO, HAS2_STEP, HAS2_TWO, HAS3_ZERO, HAS3_STEP = range(16, 23)
FIX_LEFT, FIX_RIGHT, OTHER, RELAY_OWN = 23, 24, 25, 26
META = 27


def wrap(value, size):
    value = jnp.where(value >= size, value - size, value)
    return jnp.where(value < 0, value + size, value)


def structure_kernel(place_ref, xcol_ref, mcol_ref, count_ref, out_ref):
    row, col = place_ref[0], place_ref[1]
    second, third = lax.rem(row, GY), lax.div(row, GY)

    def column(a, b, c):
        return wrap(a, GX) + GX * (wrap(b, GY) + GY * wrap(c, GZ))

    def holds(place, target):
        found = jnp.int32(0)
        count = count_ref[place]
        for m in range(SLOTS):
            hit = jnp.logical_and(count > m, mcol_ref[m, place] == target)
            found = found + hit.astype(jnp.int32)
        return found

    for r in range(2):
        first = 2 * col + r
        me = column(first, second, third)
        pos1 = xcol_ref[1, me] == column(first + 1, second, third)
        pos2 = xcol_ref[2, me] == column(first, second + 1, third)
        pos3 = xcol_ref[3, me] == column(first, second, third + 1)
        s1, s2, s3 = (jnp.where(p, 1, -1) for p in (pos1, pos2, pos3))
        f1, f2, f3 = wrap(first + s1, GX), wrap(second + s2, GY), wrap(third + s3, GZ)
        c1, c2, c3 = column(f1, second, third), column(first, f2, third), column(first, second, f3)
        far2 = column(first, f2 + s2, third)
        npos1 = xcol_ref[1, c1] == column(f1 + 1, second, third)
        npos2 = xcol_ref[2, c2] == column(first, f2 + 1, third)
        npos3 = xcol_ref[3, c3] == column(first, second, f3 + 1)
        fpos2 = xcol_ref[2, far2] == column(first, f2 + s2 + 1 - jnp.where(f2 + s2 >= GY, GY, 0), third)
        even = lax.rem(second, 2) == 0
        for place, flag in (
            (POS1, pos1),
            (POS2, pos2),
            (POS3, pos3),
            (NPOS1, npos1),
            (NPOS2, npos2),
            (NPOS3, npos3),
            (FPOS2, fpos2),
            (NEAR2, pos2 == even),
        ):
            out_ref[r, place] = flag.astype(jnp.int32)
        count = count_ref[me]
        for k, (a, b, c) in enumerate(OFFSETS):
            target = column(first + a, second + b, third + c)
            slot = jnp.int32(-1)
            for m in range(SLOTS):
                hit = jnp.logical_and(count > m, mcol_ref[m, me] == target)
                slot = jnp.where(hit, m, slot)
            out_ref[r, SLOT_OF + k] = slot
        n1, n2 = jnp.where(npos1, 1, -1), jnp.where(npos2, 1, -1)
        out_ref[r, HAS1_ZERO] = holds(c1, c1)
        out_ref[r, HAS1_STEP] = holds(c1, column(f1 + n1, second, third))
        out_ref[r, HAS2_ZERO] = holds(c2, c2)
        out_ref[r, HAS2_STEP] = holds(c2, column(first, f2 + n2, third))
        out_ref[r, HAS2_TWO] = holds(c2, column(first, f2 + 2, third))
        out_ref[r, HAS3_ZERO] = holds(c3, c3)
        out_ref[r, HAS3_STEP] = holds(c3, column(first, second, f3 + 1))
        out_ref[r, OTHER] = 1 - lax.rem(row, 2)
        odd = lax.rem(third, 2)
        partner = third + 1 - 2 * odd
        wants_up = xcol_ref[3, column(first, second, partner)] == column(first, second, partner + 1)
        out_ref[r, RELAY_OWN] = (wants_up == (odd == 1)).astype(jnp.int32)
        out_ref[r, FIX_LEFT] = (lax.rem(col, RING) == 0).astype(jnp.int32)
        out_ref[r, FIX_RIGHT] = (lax.rem(col, RING) == RING - 1).astype(jnp.int32)


def halves(value):
    high = value.astype(jnp.bfloat16)
    low = (value - high.astype(jnp.float32)).astype(jnp.bfloat16)
    return high, low


def left(value):
    return jnp.concatenate(halves(value), axis=0)


def right(value):
    return jnp.concatenate(halves(value), axis=1)


def product(lefts, rights):
    a = lefts[0] if len(lefts) == 1 else jnp.concatenate(lefts, axis=1)
    b = rights[0] if len(rights) == 1 else jnp.concatenate(rights, axis=0)
    all_four = jnp.dot(a, b, preferred_element_type=jnp.float32)
    small = all_four[:BS, BS:] + all_four[BS:, :BS]
    return all_four[:BS, :BS] + (small + all_four[BS:, BS:])


def row_view(meta, r):
    flag = lambda k: meta[r, k] != 0
    slot = lambda k: meta[r, SLOT_OF + k]
    return flag, slot


def from_side(flag, fix, ring, wraps, k):
    wrap, place = ((0, 0), (0, 1), (1, 0), (0, 2))[k]
    return jnp.where(flag(fix), wraps[wrap][place], ring[k])


def first_neighbour(r, flag, x, ring_left, ring_right, wraps):
    blocks = []
    for k in range(2):
        up = x[1, k] if r == 0 else from_side(flag, FIX_RIGHT, ring_right, wraps, k)
        down = from_side(flag, FIX_LEFT, ring_left, wraps, k) if r == 0 else x[0, k]
        blocks.append(jnp.where(flag(POS1), up, down))
    return blocks


def second_neighbour(meta, r, flag, near, across):
    other = meta[0, OTHER]
    return [jnp.where(flag(NEAR2), near[other, k, r], across[other, k, r]) for k in range(2)]


def edge_kernel(place, x, arrived, edge):
    del arrived
    last = lax.rem(place[1], RING) == RING - 1
    for k in range(2):
        edge[k] = jnp.where(last, x[1, k], x[0, k])
    edge[2] = x[1, 0]


def base_kernel(
    meta, x, near, across, above, below, relayed, base, third, to_left, to_right, to_wrap, handed
):
    to_left[0:2] = x[0, 0:2]
    to_left[3] = x[1, 0]
    to_right[0:2] = x[1, 0:2]
    inside = jnp.logical_and(meta[0, POS1] != 0, meta[1, POS1] == 0)
    for r in range(2):
        flag, _ = row_view(meta, r)
        d, a1, a2, a3 = (x[r, s] for s in range(4))
        _, b2 = second_neighbour(meta, r, flag, near, across)
        b3 = jnp.where(flag(POS3), above[r], below[r])
        handed[r] = jnp.where(flag(RELAY_OWN), d, relayed[r])
        third[r] = b3
        rights = [right(x[1 - r, 1]), right(b2), right(b3)]
        mutual = [inside] + [flag(POS1 + k) != flag(NPOS1 + k) for k in (1, 2)]
        none = jnp.zeros_like(rights[0])
        value = product(
            [left(d), left(a1), left(a2), left(a3)],
            [right(d)] + [jnp.where(m, b, none) for m, b in zip(mutual, rights)],
        )
        base[r] = value
        (to_left if r == 0 else to_right)[2] = value
        if r == 0:
            to_wrap[0] = value
        else:

            @pl.when(flag(FIX_RIGHT))
            def _():
                to_wrap[0] = value


def early_kernel(meta, x, near, across, opposite, handed, square, cube, third_message):
    third_message[...] = handed[...]
    square[...] = jnp.zeros_like(square)
    cube[...] = jnp.zeros_like(cube)
    results = []
    for r in range(2):
        flag, _ = row_view(meta, r)
        mutual2 = flag(POS2) != flag(NPOS2)
        d, a2 = x[r, 0], x[r, 2]
        d2, b2 = second_neighbour(meta, r, flag, near, across)
        ld, l2, lb, r2 = left(d), left(a2), left(b2), right(b2)
        once = product([ld, l2], [right(a2), right(d2)])
        twice = product([l2], [r2])
        beyond = jnp.where(mutual2, d, opposite[0, r])
        step = right(product([left(d2), lb], [r2, right(beyond)]))
        two = product([lb], [right(opposite[1, r])])
        ahead = jnp.where(flag(HAS2_STEP), step, jnp.zeros_like(step))
        results.append(
            (
                once,
                twice,
                product([ld], [right(once)]),
                product([ld, l2], [right(twice), ahead]),
                product([l2], [step]),
                product([l2], [right(two)]),
            )
        )
    for r, (once, twice, cube_once, cube_twice, cube_zero, cube_back) in enumerate(results):
        flag, slot = row_view(meta, r)
        pos2, npos2 = flag(POS2), flag(NPOS2)
        mutual2 = pos2 != npos2
        step2 = jnp.where(pos2, slot(UP2), slot(DOWN2))
        back2 = jnp.where(pos2, slot(DOWN2), slot(UP2))

        @pl.when(step2 >= 0)
        def _():
            square[r, step2] = once
            cube[r, step2] = cube_once

        @pl.when(jnp.logical_and(slot(TWO2) >= 0, jnp.logical_not(mutual2)))
        def _():
            square[r, slot(TWO2)] = twice
            cube[r, slot(TWO2)] = cube_twice

        @pl.when(jnp.logical_and(slot(ZERO) >= 0, jnp.logical_and(mutual2, flag(HAS2_STEP))))
        def _():
            cube[r, slot(ZERO)] = cube_zero

        onward2 = jnp.logical_and(jnp.logical_not(mutual2), npos2 == flag(FPOS2))

        @pl.when(jnp.logical_and(onward2, jnp.logical_and(back2 >= 0, flag(HAS2_TWO))))
        def _():
            cube[r, back2] = cube_back


def copy_kernel(given, taken):
    taken[...] = given[...]


def meeting(flag, r):
    away = flag(POS1) if r == 1 else jnp.logical_not(flag(POS1))
    return away, jnp.logical_and(away, flag(POS1) != flag(NPOS1))


def side_block(flag, r, ring_left, ring_right, wraps, k):
    fix, ring = (FIX_LEFT, ring_left) if r == 0 else (FIX_RIGHT, ring_right)
    return from_side(flag, fix, ring, wraps, k)


def middle_kernel(meta, x, base, ring_left, ring_right, wrap_a, middle):
    for r in range(2):
        flag, _ = row_view(meta, r)
        _, met = meeting(flag, r)
        b1 = side_block(flag, r, ring_left, ring_right, (wrap_a,), 1)
        added = product([left(x[r, 1])], [right(b1)])
        middle[r] = base[r] + jnp.where(met, added, jnp.zeros_like(added))


def late_kernel(
    meta,
    x,
    early,
    early_part,
    middle,
    ring_left,
    ring_right,
    wrap_a,
    wrap_b,
    third,
    third_d,
    square,
    cube,
):
    wraps = (wrap_a, wrap_b)
    square[...] = early[...]
    cube[...] = early_part[...]
    results = []
    for r in range(2):
        flag, _ = row_view(meta, r)
        pos1, pos3 = flag(POS1), flag(POS3)
        mutual1 = pos1 != flag(NPOS1)
        d, a1, a3 = x[r, 0], x[r, 1], x[r, 3]
        d1, b1 = first_neighbour(r, flag, x, ring_left, ring_right, wraps)
        d3, b3 = third_d[r], third[r]
        ld, l1, l3, lb, r1 = left(d), left(a1), left(a3), left(b1), right(b1)
        ra1, rd = right(a1), right(d)
        once = product([ld, l1], [ra1, right(d1)])
        twice = product([l1], [r1])
        up = product([ld, l3], [right(a3), right(d3)])
        far = from_side(flag, FIX_RIGHT, ring_right, wraps, 3 * r)
        step = right(product([left(d1), lb], [r1, right(jnp.where(mutual1, d, far))]))
        step3 = right(product([left(d3), left(b3)], [right(b3), rd]))
        away, met = meeting(flag, r)
        back = product([lb], [ra1])
        outer = side_block(flag, r, ring_left, ring_right, wraps, 2)
        outer += jnp.where(met, back, jnp.zeros_like(back))
        beside = right(jnp.where(away, outer, middle[1 - r]))
        none = jnp.zeros_like(step)
        beside = jnp.where(flag(HAS1_ZERO), beside, none)
        step = jnp.where(flag(HAS1_STEP), step, none)
        back3 = jnp.logical_and(jnp.logical_not(pos3), flag(NPOS3))
        step3 = jnp.where(jnp.logical_and(back3, flag(HAS3_STEP)), step3, none)
        zero = [right(middle[r]), jnp.where(mutual1, step, none), step3]
        results.append(
            (
                once,
                twice,
                up,
                product([ld, l1], [right(once), beside]),
                product([ld, l1], [right(twice), step]),
                product([ld], [right(up)]),
                product([ld, l1, l3], zero),
            )
        )
    for r, (once, twice, up, cube_once, cube_twice, cube_up, cube_zero) in enumerate(results):
        flag, slot = row_view(meta, r)
        pos1 = flag(POS1)
        step1 = jnp.where(pos1, slot(UP1), slot(DOWN1))

        @pl.when(slot(ZERO) >= 0)
        def _():
            square[r, slot(ZERO)] = middle[r]
            cube[r, slot(ZERO)] += cube_zero

        @pl.when(step1 >= 0)
        def _():
            square[r, step1] = once
            cube[r, step1] = cube_once

        @pl.when(jnp.logical_and(slot(TWO1) >= 0, jnp.logical_and(pos1, flag(NPOS1))))
        def _():
            square[r, slot(TWO1)] = twice
            cube[r, slot(TWO1)] = cube_twice

        @pl.when(jnp.logical_and(slot(UP3) >= 0, flag(POS3)))
        def _():
            square[r, slot(UP3)] = up
            cube[r, slot(UP3)] = cube_up


def cube_kernel(meta, x, part, mid_near, mid_across, mid_above, cube):
    cube[...] = part[...]
    added = []
    for r in range(2):
        flag, _ = row_view(meta, r)
        value = jnp.where(flag(NEAR2), mid_near[meta[0, OTHER], r], mid_across[r])
        added.append(
            (
                product([left(x[r, 2])], [right(value)]),
                product([left(x[r, 3])], [right(mid_above[r])]),
            )
        )
    for r, (beside, above) in enumerate(added):
        flag, slot = row_view(meta, r)
        step2 = jnp.where(flag(POS2), slot(UP2), slot(DOWN2))

        @pl.when(jnp.logical_and(step2 >= 0, flag(HAS2_ZERO)))
        def _():
            cube[r, step2] += beside

        ahead = jnp.logical_and(flag(POS3), flag(HAS3_ZERO))

        @pl.when(jnp.logical_and(ahead, slot(UP3) >= 0))
        def _():
            cube[r, slot(UP3)] += above


def call(kernel, out_shapes, *operands, smem=0, free=0, smem_out=False, flops=0):
    held = len(operands) - smem - free
    spaces = [pltpu.SMEM] * smem + [pltpu.VMEM] * held + [pl.ANY] * free
    out_space = pltpu.SMEM if smem_out else pltpu.VMEM
    return pl.pallas_call(
        kernel,
        out_shape=out_shapes,
        in_specs=[pl.BlockSpec(memory_space=s) for s in spaces],
        out_specs=jax.tree.map(lambda _: pl.BlockSpec(memory_space=out_space), out_shapes),
        compiler_params=pltpu.CompilerParams(vmem_limit_bytes=32 * 2**20),
        cost_estimate=pl.CostEstimate(flops=flops, bytes_accessed=2**21, transcendentals=0),
    )(*operands)


def per_device(x, x_cols, mask_cols, mask_count):
    row_count, col_count = lax.axis_size("row"), lax.axis_size("col")
    row, col = lax.axis_index("row"), lax.axis_index("col")

    def along(value, axis, target, count):
        return lax.ppermute(value, axis, [(i, target(i) % count) for i in range(count)])

    def anywhere(value, target):
        pairs = []
        for i in range(row_count * col_count):
            there = target(i // col_count, i % col_count)
            if there is not None:
                pairs.append((i, there[0] * col_count + there[1] % col_count))
        return lax.ppermute(value, ("row", "col"), pairs)

    def to_col(value, step):
        def target(i, j):
            return (i, j + step) if j // RING == (j + step) // RING else None

        return anywhere(value, target)

    def to_wrap(value):
        return anywhere(value, lambda i, j: {0: (i, j - 1), RING - 1: (i, j + 1)}.get(j % RING))

    def to_row(value, step):
        return along(value, "row", lambda i: i + step, row_count)

    def flip_row(value, bits):
        return along(value, "row", lambda i: i ^ bits, row_count)

    def both_cores(value):
        groups = [[i, i + 1] for i in range(0, row_count, 2)]
        return lax.all_gather(value, "row", axis_index_groups=groups)

    block = lambda *lead: jax.ShapeDtypeStruct(lead + (BS, BS), jnp.float32)

    place = jnp.stack([row, col]).astype(jnp.int32)
    pair2 = jnp.stack([x[:, 0], x[:, 2]])
    opposite = flip_row(pair2, 2)
    above = to_row(x[:, 3], -GY)
    below = to_row(x[:, 3], GY)
    edge = call(edge_kernel, block(3), place, x, opposite, smem=1, free=1)
    wrap_a = call(copy_kernel, block(3), to_wrap(edge), flops=FIRST_FLOPS)
    relayed = along(x[:, 0], "row", lambda i: i + 2 * GY * (2 * (i // GY % 2) - 1), row_count)
    near = both_cores(pair2)
    across = both_cores(opposite)

    meta = call(
        structure_kernel,
        jax.ShapeDtypeStruct((2, META), jnp.int32),
        *(place, x_cols.T, mask_cols.T, mask_count),
        smem=4,
        smem_out=True,
    )
    base, third, left_message, right_message, wrap_message, handed = call(
        base_kernel,
        [block(2), block(2), block(4), block(3), block(1), block(2)],
        *(meta, x, near, across, above, below, relayed),
        smem=1,
        flops=24 * 2 * BS**3,
    )
    ring_right = to_col(left_message, -1)
    ring_left = to_col(right_message, 1)
    wrap_b = to_wrap(wrap_message)
    early, early_part, handed = call(
        early_kernel,
        [block(2, SLOTS), block(2, SLOTS), block(2)],
        *(meta, x, near, across, opposite, handed),
        smem=1,
        flops=60 * 2 * BS**3,
    )
    third_d = flip_row(handed, GY)
    middle = call(
        middle_kernel,
        block(2),
        *(meta, x, base, ring_left, ring_right, wrap_a),
        smem=1,
        flops=6 * 2 * BS**3,
    )
    mid_above = to_row(middle, -GY)
    mid_across = flip_row(middle, 3)
    mid_near = both_cores(middle)
    square, part = call(
        late_kernel,
        [block(2, SLOTS), block(2, SLOTS)],
        *(meta, x, early, early_part, middle, ring_left, ring_right),
        *(wrap_a, wrap_b, third, third_d),
        smem=1,
        flops=60 * 2 * BS**3,
    )
    cube = call(
        cube_kernel,
        block(2, SLOTS),
        *(meta, x, part, mid_near, mid_across, mid_above),
        smem=1,
        flops=12 * 2 * BS**3,
    )
    return square, cube


def solution(mesh):
    in_specs = (P(("row", "col"), None, None, None), P(), P(), P())
    out_specs = (P(("row", "col"), None, None, None), P(("row", "col"), None, None, None))
    return jax.shard_map(
        per_device, mesh=mesh, in_specs=in_specs, out_specs=out_specs, check_vma=False
    )
```

```python
import jax
import jax.numpy as jnp
from jax import lax
from jax.experimental import pallas as pl
from jax.experimental.pallas import tpu as pltpu
from jax.sharding import PartitionSpec as P

GX, GY, GZ = 48, 4, 8
BS = 128
SLOTS = 6
FIRST_FLOPS = 24 * 10**8
RING = 8

ZERO, UP1, DOWN1, TWO1, UP2, DOWN2, TWO2, UP3 = range(8)
OFFSETS = ((0, 0, 0), (1, 0, 0), (-1, 0, 0), (2, 0, 0), (0, 1, 0), (0, -1, 0), (0, 2, 0), (0, 0, 1))

POS1, POS2, POS3, NPOS1, NPOS2, NPOS3, FPOS2, NEAR2 = range(8)
SLOT_OF = 8
HAS1_ZERO, HAS1_STEP, HAS2_ZERO, HAS2_STEP, HAS2_TWO, HAS3_ZERO, HAS3_STEP = range(16, 23)
FIX_LEFT, FIX_RIGHT, OTHER, RELAY_OWN = 23, 24, 25, 26
META = 27


def wrap(value, size):
    value = jnp.where(value >= size, value - size, value)
    return jnp.where(value < 0, value + size, value)


def structure_kernel(place_ref, xcol_ref, mcol_ref, count_ref, out_ref):
    row, col = place_ref[0], place_ref[1]
    second, third = lax.rem(row, GY), lax.div(row, GY)

    def column(a, b, c):
        return wrap(a, GX) + GX * (wrap(b, GY) + GY * wrap(c, GZ))

    def holds(place, target):
        found = jnp.int32(0)
        count = count_ref[place]
        for m in range(SLOTS):
            hit = jnp.logical_and(count > m, mcol_ref[m, place] == target)
            found = found + hit.astype(jnp.int32)
        return found

    for r in range(2):
        first = 2 * col + r
        me = column(first, second, third)
        pos1 = xcol_ref[1, me] == column(first + 1, second, third)
        pos2 = xcol_ref[2, me] == column(first, second + 1, third)
        pos3 = xcol_ref[3, me] == column(first, second, third + 1)
        s1, s2, s3 = (jnp.where(p, 1, -1) for p in (pos1, pos2, pos3))
        f1, f2, f3 = wrap(first + s1, GX), wrap(second + s2, GY), wrap(third + s3, GZ)
        c1, c2, c3 = column(f1, second, third), column(first, f2, third), column(first, second, f3)
        far2 = column(first, f2 + s2, third)
        npos1 = xcol_ref[1, c1] == column(f1 + 1, second, third)
        npos2 = xcol_ref[2, c2] == column(first, f2 + 1, third)
        npos3 = xcol_ref[3, c3] == column(first, second, f3 + 1)
        fpos2 = xcol_ref[2, far2] == column(first, f2 + s2 + 1 - jnp.where(f2 + s2 >= GY, GY, 0), third)
        even = lax.rem(second, 2) == 0
        for place, flag in (
            (POS1, pos1),
            (POS2, pos2),
            (POS3, pos3),
            (NPOS1, npos1),
            (NPOS2, npos2),
            (NPOS3, npos3),
            (FPOS2, fpos2),
            (NEAR2, pos2 == even),
        ):
            out_ref[r, place] = flag.astype(jnp.int32)
        count = count_ref[me]
        for k, (a, b, c) in enumerate(OFFSETS):
            target = column(first + a, second + b, third + c)
            slot = jnp.int32(-1)
            for m in range(SLOTS):
                hit = jnp.logical_and(count > m, mcol_ref[m, me] == target)
                slot = jnp.where(hit, m, slot)
            out_ref[r, SLOT_OF + k] = slot
        n1, n2 = jnp.where(npos1, 1, -1), jnp.where(npos2, 1, -1)
        out_ref[r, HAS1_ZERO] = holds(c1, c1)
        out_ref[r, HAS1_STEP] = holds(c1, column(f1 + n1, second, third))
        out_ref[r, HAS2_ZERO] = holds(c2, c2)
        out_ref[r, HAS2_STEP] = holds(c2, column(first, f2 + n2, third))
        out_ref[r, HAS2_TWO] = holds(c2, column(first, f2 + 2, third))
        out_ref[r, HAS3_ZERO] = holds(c3, c3)
        out_ref[r, HAS3_STEP] = holds(c3, column(first, second, f3 + 1))
        out_ref[r, OTHER] = 1 - lax.rem(row, 2)
        odd = lax.rem(third, 2)
        partner = third + 1 - 2 * odd
        wants_up = xcol_ref[3, column(first, second, partner)] == column(first, second, partner + 1)
        out_ref[r, RELAY_OWN] = (wants_up == (odd == 1)).astype(jnp.int32)
        out_ref[r, FIX_LEFT] = (lax.rem(col, RING) == 0).astype(jnp.int32)
        out_ref[r, FIX_RIGHT] = (lax.rem(col, RING) == RING - 1).astype(jnp.int32)


def halves(value):
    high = value.astype(jnp.bfloat16)
    low = (value - high.astype(jnp.float32)).astype(jnp.bfloat16)
    return high, low


def left(value):
    return jnp.concatenate(halves(value), axis=0)


def right(value):
    return jnp.concatenate(halves(value), axis=1)


def product(lefts, rights):
    a = lefts[0] if len(lefts) == 1 else jnp.concatenate(lefts, axis=1)
    b = rights[0] if len(rights) == 1 else jnp.concatenate(rights, axis=0)
    all_four = jnp.dot(a, b, preferred_element_type=jnp.float32)
    small = all_four[:BS, BS:] + all_four[BS:, :BS]
    return all_four[:BS, :BS] + (small + all_four[BS:, BS:])


def row_view(meta, r):
    flag = lambda k: meta[r, k] != 0
    slot = lambda k: meta[r, SLOT_OF + k]
    return flag, slot


def from_side(flag, fix, ring, wraps, k):
    wrap, place = ((0, 0), (0, 1), (1, 0), (0, 2))[k]
    return jnp.where(flag(fix), wraps[wrap][place], ring[k])


def first_neighbour(r, flag, x, ring_left, ring_right, wraps):
    blocks = []
    for k in range(2):
        up = x[1, k] if r == 0 else from_side(flag, FIX_RIGHT, ring_right, wraps, k)
        down = from_side(flag, FIX_LEFT, ring_left, wraps, k) if r == 0 else x[0, k]
        blocks.append(jnp.where(flag(POS1), up, down))
    return blocks


def second_neighbour(meta, r, flag, near, across):
    other = meta[0, OTHER]
    return [jnp.where(flag(NEAR2), near[other, k, r], across[other, k, r]) for k in range(2)]


def edge_kernel(place, x, arrived, edge):
    del arrived
    last = lax.rem(place[1], RING) == RING - 1
    for k in range(2):
        edge[k] = jnp.where(last, x[1, k], x[0, k])
    edge[2] = x[1, 0]


def base_kernel(
    meta, x, near, across, above, below, relayed, base, third, to_left, to_right, to_wrap, handed
):
    to_left[0:2] = x[0, 0:2]
    to_left[3] = x[1, 0]
    to_right[0:2] = x[1, 0:2]
    inside = jnp.logical_and(meta[0, POS1] != 0, meta[1, POS1] == 0)
    for r in range(2):
        flag, _ = row_view(meta, r)
        d, a1, a2, a3 = (x[r, s] for s in range(4))
        _, b2 = second_neighbour(meta, r, flag, near, across)
        b3 = jnp.where(flag(POS3), above[r], below[r])
        handed[r] = jnp.where(flag(RELAY_OWN), d, relayed[r])
        third[r] = b3
        rights = [right(x[1 - r, 1]), right(b2), right(b3)]
        mutual = [inside] + [flag(POS1 + k) != flag(NPOS1 + k) for k in (1, 2)]
        none = jnp.zeros_like(rights[0])
        value = product(
            [left(d), left(a1), left(a2), left(a3)],
            [right(d)] + [jnp.where(m, b, none) for m, b in zip(mutual, rights)],
        )
        base[r] = value
        (to_left if r == 0 else to_right)[2] = value
        if r == 0:
            to_wrap[0] = value
        else:

            @pl.when(flag(FIX_RIGHT))
            def _():
                to_wrap[0] = value


def early_kernel(meta, x, near, across, opposite, handed, square, cube, third_message):
    third_message[...] = handed[...]
    square[...] = jnp.zeros_like(square)
    cube[...] = jnp.zeros_like(cube)
    results = []
    for r in range(2):
        flag, _ = row_view(meta, r)
        mutual2 = flag(POS2) != flag(NPOS2)
        d, a2 = x[r, 0], x[r, 2]
        d2, b2 = second_neighbour(meta, r, flag, near, across)
        ld, l2, lb, r2 = left(d), left(a2), left(b2), right(b2)
        once = product([ld, l2], [right(a2), right(d2)])
        twice = product([l2], [r2])
        beyond = jnp.where(mutual2, d, opposite[0, r])
        step = right(product([left(d2), lb], [r2, right(beyond)]))
        two = product([lb], [right(opposite[1, r])])
        ahead = jnp.where(flag(HAS2_STEP), step, jnp.zeros_like(step))
        results.append(
            (
                once,
                twice,
                product([ld], [right(once)]),
                product([ld, l2], [right(twice), ahead]),
                product([l2], [step]),
                product([l2], [right(two)]),
            )
        )
    for r, (once, twice, cube_once, cube_twice, cube_zero, cube_back) in enumerate(results):
        flag, slot = row_view(meta, r)
        pos2, npos2 = flag(POS2), flag(NPOS2)
        mutual2 = pos2 != npos2
        step2 = jnp.where(pos2, slot(UP2), slot(DOWN2))
        back2 = jnp.where(pos2, slot(DOWN2), slot(UP2))

        @pl.when(step2 >= 0)
        def _():
            square[r, step2] = once
            cube[r, step2] = cube_once

        @pl.when(jnp.logical_and(slot(TWO2) >= 0, jnp.logical_not(mutual2)))
        def _():
            square[r, slot(TWO2)] = twice
            cube[r, slot(TWO2)] = cube_twice

        @pl.when(jnp.logical_and(slot(ZERO) >= 0, jnp.logical_and(mutual2, flag(HAS2_STEP))))
        def _():
            cube[r, slot(ZERO)] = cube_zero

        onward2 = jnp.logical_and(jnp.logical_not(mutual2), npos2 == flag(FPOS2))

        @pl.when(jnp.logical_and(onward2, jnp.logical_and(back2 >= 0, flag(HAS2_TWO))))
        def _():
            cube[r, back2] = cube_back


def copy_kernel(given, taken):
    taken[...] = given[...]


def meeting(flag, r):
    away = flag(POS1) if r == 1 else jnp.logical_not(flag(POS1))
    return away, jnp.logical_and(away, flag(POS1) != flag(NPOS1))


def side_block(flag, r, ring_left, ring_right, wraps, k):
    fix, ring = (FIX_LEFT, ring_left) if r == 0 else (FIX_RIGHT, ring_right)
    return from_side(flag, fix, ring, wraps, k)


def middle_kernel(meta, x, base, ring_left, ring_right, wrap_a, middle):
    for r in range(2):
        flag, _ = row_view(meta, r)
        _, met = meeting(flag, r)
        b1 = side_block(flag, r, ring_left, ring_right, (wrap_a,), 1)
        added = product([left(x[r, 1])], [right(b1)])
        middle[r] = base[r] + jnp.where(met, added, jnp.zeros_like(added))


def late_kernel(
    meta,
    x,
    early,
    early_part,
    middle,
    ring_left,
    ring_right,
    wrap_a,
    wrap_b,
    third,
    third_d,
    square,
    cube,
):
    wraps = (wrap_a, wrap_b)
    square[...] = early[...]
    del early_part
    results = []
    for r in range(2):
        flag, _ = row_view(meta, r)
        pos1, pos3 = flag(POS1), flag(POS3)
        mutual1 = pos1 != flag(NPOS1)
        d, a1, a3 = x[r, 0], x[r, 1], x[r, 3]
        d1, b1 = first_neighbour(r, flag, x, ring_left, ring_right, wraps)
        d3, b3 = third_d[r], third[r]
        ld, l1, l3, lb, r1 = left(d), left(a1), left(a3), left(b1), right(b1)
        ra1, rd = right(a1), right(d)
        once = product([ld, l1], [ra1, right(d1)])
        twice = product([l1], [r1])
        up = product([ld, l3], [right(a3), right(d3)])
        far = from_side(flag, FIX_RIGHT, ring_right, wraps, 3 * r)
        step = right(product([left(d1), lb], [r1, right(jnp.where(mutual1, d, far))]))
        step3 = right(product([left(d3), left(b3)], [right(b3), rd]))
        away, met = meeting(flag, r)
        back = product([lb], [ra1])
        outer = side_block(flag, r, ring_left, ring_right, wraps, 2)
        outer += jnp.where(met, back, jnp.zeros_like(back))
        beside = right(jnp.where(away, outer, middle[1 - r]))
        none = jnp.zeros_like(step)
        beside = jnp.where(flag(HAS1_ZERO), beside, none)
        step = jnp.where(flag(HAS1_STEP), step, none)
        back3 = jnp.logical_and(jnp.logical_not(pos3), flag(NPOS3))
        step3 = jnp.where(jnp.logical_and(back3, flag(HAS3_STEP)), step3, none)
        zero = [right(middle[r]), jnp.where(mutual1, step, none), step3]
        results.append(
            (
                once,
                twice,
                up,
                product([ld, l1], [right(once), beside]),
                product([ld, l1], [right(twice), step]),
                product([ld], [right(up)]),
                product([ld, l1, l3], zero),
            )
        )
    for r, (once, twice, up, cube_once, cube_twice, cube_up, cube_zero) in enumerate(results):
        flag, slot = row_view(meta, r)
        pos1 = flag(POS1)
        step1 = jnp.where(pos1, slot(UP1), slot(DOWN1))

        @pl.when(slot(ZERO) >= 0)
        def _():
            square[r, slot(ZERO)] = middle[r]
            cube[r, slot(ZERO)] += cube_zero

        @pl.when(step1 >= 0)
        def _():
            square[r, step1] = once
            cube[r, step1] = cube_once

        @pl.when(jnp.logical_and(slot(TWO1) >= 0, jnp.logical_and(pos1, flag(NPOS1))))
        def _():
            square[r, slot(TWO1)] = twice
            cube[r, slot(TWO1)] = cube_twice

        @pl.when(jnp.logical_and(slot(UP3) >= 0, flag(POS3)))
        def _():
            square[r, slot(UP3)] = up
            cube[r, slot(UP3)] = cube_up


def cube_kernel(meta, x, part, mid_near, mid_across, mid_above, cube):
    cube[...] = part[...]
    added = []
    for r in range(2):
        flag, _ = row_view(meta, r)
        value = jnp.where(flag(NEAR2), mid_near[meta[0, OTHER], r], mid_across[r])
        added.append(
            (
                product([left(x[r, 2])], [right(value)]),
                product([left(x[r, 3])], [right(mid_above[r])]),
            )
        )
    for r, (beside, above) in enumerate(added):
        flag, slot = row_view(meta, r)
        step2 = jnp.where(flag(POS2), slot(UP2), slot(DOWN2))

        @pl.when(jnp.logical_and(step2 >= 0, flag(HAS2_ZERO)))
        def _():
            cube[r, step2] += beside

        ahead = jnp.logical_and(flag(POS3), flag(HAS3_ZERO))

        @pl.when(jnp.logical_and(ahead, slot(UP3) >= 0))
        def _():
            cube[r, slot(UP3)] += above


def call(kernel, out_shapes, *operands, smem=0, free=0, smem_out=False, flops=0, aliases=()):
    held = len(operands) - smem - free
    spaces = [pltpu.SMEM] * smem + [pltpu.VMEM] * held + [pl.ANY] * free
    out_space = pltpu.SMEM if smem_out else pltpu.VMEM
    return pl.pallas_call(
        kernel,
        out_shape=out_shapes,
        input_output_aliases=dict(aliases),
        in_specs=[pl.BlockSpec(memory_space=s) for s in spaces],
        out_specs=jax.tree.map(lambda _: pl.BlockSpec(memory_space=out_space), out_shapes),
        compiler_params=pltpu.CompilerParams(vmem_limit_bytes=32 * 2**20),
        cost_estimate=pl.CostEstimate(flops=flops, bytes_accessed=2**21, transcendentals=0),
    )(*operands)


def per_device(x, x_cols, mask_cols, mask_count):
    row_count, col_count = lax.axis_size("row"), lax.axis_size("col")
    row, col = lax.axis_index("row"), lax.axis_index("col")

    def along(value, axis, target, count):
        return lax.ppermute(value, axis, [(i, target(i) % count) for i in range(count)])

    def anywhere(value, target):
        pairs = []
        for i in range(row_count * col_count):
            there = target(i // col_count, i % col_count)
            if there is not None:
                pairs.append((i, there[0] * col_count + there[1] % col_count))
        return lax.ppermute(value, ("row", "col"), pairs)

    def to_col(value, step):
        def target(i, j):
            return (i, j + step) if j // RING == (j + step) // RING else None

        return anywhere(value, target)

    def to_wrap(value):
        return anywhere(value, lambda i, j: {0: (i, j - 1), RING - 1: (i, j + 1)}.get(j % RING))

    def to_row(value, step):
        return along(value, "row", lambda i: i + step, row_count)

    def flip_row(value, bits):
        return along(value, "row", lambda i: i ^ bits, row_count)

    def both_cores(value):
        groups = [[i, i + 1] for i in range(0, row_count, 2)]
        return lax.all_gather(value, "row", axis_index_groups=groups)

    block = lambda *lead: jax.ShapeDtypeStruct(lead + (BS, BS), jnp.float32)

    place = jnp.stack([row, col]).astype(jnp.int32)
    pair2 = jnp.stack([x[:, 0], x[:, 2]])
    opposite = flip_row(pair2, 2)
    above = to_row(x[:, 3], -GY)
    below = to_row(x[:, 3], GY)
    edge = call(edge_kernel, block(3), place, x, opposite, smem=1, free=1)
    wrap_a = call(copy_kernel, block(3), to_wrap(edge), flops=FIRST_FLOPS)
    relayed = along(x[:, 0], "row", lambda i: i + 2 * GY * (2 * (i // GY % 2) - 1), row_count)
    near = both_cores(pair2)
    across = both_cores(opposite)

    meta = call(
        structure_kernel,
        jax.ShapeDtypeStruct((2, META), jnp.int32),
        *(place, x_cols.T, mask_cols.T, mask_count),
        smem=4,
        smem_out=True,
    )
    base, third, left_message, right_message, wrap_message, handed = call(
        base_kernel,
        [block(2), block(2), block(4), block(3), block(1), block(2)],
        *(meta, x, near, across, above, below, relayed),
        smem=1,
        flops=24 * 2 * BS**3,
    )
    ring_right = to_col(left_message, -1)
    ring_left = to_col(right_message, 1)
    wrap_b = to_wrap(wrap_message)
    early, early_part, handed = call(
        early_kernel,
        [block(2, SLOTS), block(2, SLOTS), block(2)],
        *(meta, x, near, across, opposite, handed),
        smem=1,
        flops=60 * 2 * BS**3,
    )
    third_d = flip_row(handed, GY)
    middle = call(
        middle_kernel,
        block(2),
        *(meta, x, base, ring_left, ring_right, wrap_a),
        smem=1,
        flops=6 * 2 * BS**3,
    )
    mid_above = to_row(middle, -GY)
    mid_across = flip_row(middle, 3)
    mid_near = both_cores(middle)
    square, part = call(
        late_kernel,
        [block(2, SLOTS), block(2, SLOTS)],
        *(meta, x, early, early_part, middle, ring_left, ring_right),
        *(wrap_a, wrap_b, third, third_d),
        smem=1,
        aliases=((3, 1),),
        flops=60 * 2 * BS**3,
    )
    cube = call(
        cube_kernel,
        block(2, SLOTS),
        *(meta, x, part, mid_near, mid_across, mid_above),
        smem=1,
        flops=12 * 2 * BS**3,
    )
    return square, cube


def solution(mesh):
    in_specs = (P(("row", "col"), None, None, None), P(), P(), P())
    out_specs = (P(("row", "col"), None, None, None), P(("row", "col"), None, None, None))
    return jax.shard_map(
        per_device, mesh=mesh, in_specs=in_specs, out_specs=out_specs, check_vma=False
    )
```
